256 devices in a mesh: member: 32 (over z, y), slab: 8 (over x, core).
Axes of the slice: x: 4, y: 4, z: 8, core: 2. Of those that a mesh axis runs over, the one named last changes fastest.
Arguments:
- members: bfloat16 [64, 256, 8192], P('member', 'slab'), may hold values from -6 to 6
- direction: float32 [256, 8192], P('slab'), may hold values from -100 to 100
- residual: float32 [256, 8192], P('slab', 'member'), may hold values from -100 to 100
- iterate: float32 [256, 8192], P('slab', 'member'), may hold values from -6 to 6
- tiles: bfloat16 [64, 4, 128, 128], replicated, may hold values from -0.25 to 0.25
- columns: int32 [64, 4], replicated, may hold values from 0 to 63, as said below
- vertical: float32 [256, 9], replicated, may hold values from -2 to 2
Outputs:
- iterate_new: float32 [256, 8192], P('slab', 'member')
- residual_new: float32 [256, 8192], P('slab', 'member')
- direction_new: float32 [256, 8192], P('slab', 'member')
The draws below stay inside these ranges and needn't reach their ends.
Inputs may be any that keep to these rules, and one draw needn't show every extreme that they name: `columns`: row block r lists 4 distinct column blocks, r itself first.
All inputs are finite; a program needn't handle non-finite values.
Results may differ from the reference program's by a relative error of at most 0.00087.
Values may be sent and summed in bfloat16 or wider, within the bound.
No kernel may reach another device: no remote copies, remote signals or barrier semaphores. Data moves between devices by JAX's collectives and lax.ppermute only.
A program may use at most 64 MiB of HBM per device.

```python
import math
import jax
import jax.numpy as jnp
from jax import lax

NB = 64
BR = 4
TILE = 128
REACH = 4
MEMBERS = 64
LEV = 256
P_SIZE = 8192


def rough_field(key, spread, factor):
    key_level, key_point, key_gauss = jax.random.split(key, 3)
    points = NB * TILE
    level_pos = jnp.arange(LEV, dtype=jnp.float32) / max(LEV - 1, 1)
    point_pos = jnp.arange(points, dtype=jnp.float32) / max(points - 1, 1)
    level_scale = jnp.exp(math.log(3.0) * level_pos + jax.random.uniform(key_level, (LEV,), jnp.float32, 0.0, spread))
    point_scale = jnp.exp(math.log(3.0) * point_pos + jax.random.uniform(key_point, (points,), jnp.float32, 0.0, spread))
    gauss = jnp.clip(jax.random.normal(key_gauss, (LEV, points), jnp.float32), -4.0, 4.0)
    base = gauss
    return base * level_scale[:, None] * point_scale[None, :] * factor


def draw_direction(key, part):
    key = jax.random.fold_in(key, 11)
    return rough_field(key, 1.19, 0.125)


def draw_residual(key, part):
    key = jax.random.fold_in(key, 23)
    return rough_field(key, 1.19, 0.125)


def draw_columns(key, part):
    key = jax.random.fold_in(key, 37)
    row_keys = jax.random.split(key, NB)

    def one_row(row_key):
        return jax.random.permutation(row_key, NB - 1)[:BR - 1] + 1
    offsets = jax.vmap(one_row)(row_keys)
    offsets = jnp.concatenate([jnp.zeros((NB, 1), jnp.int32), offsets.astype(jnp.int32)], axis=1)
    rows = jnp.arange(NB, dtype=jnp.int32)[:, None]
    return ((rows + offsets) % NB).astype(jnp.int32)


def strengthened(drawn, stream_key, source, target, parts, factor):
    def block_of(dim):
        return (jnp.arange(drawn.shape[dim]) // (drawn.shape[dim] // parts)).reshape((-1,) + (1,) * (drawn.ndim - 1 - dim))

    near = jax.random.permutation(stream_key, parts)[block_of(target)]
    second = (block_of(target) + parts // 2) % parts
    return jnp.where((block_of(source) == near) | (block_of(source) == second), factor * drawn, drawn)


def block_scale(rng, shape, cuts, least, largest):
    factor_of, own = 1.0, jax.random.fold_in(rng, 6)
    for dim, shards_of in cuts:
        heights = jnp.exp(jax.random.uniform(jax.random.fold_in(own, dim), (shards_of,), jnp.float32, least / len(cuts), largest / len(cuts)))
        factor_of = factor_of * jnp.repeat(heights, shape[dim] // shards_of).reshape([-1 if axis == dim else 1 for axis in range(len(shape))])
    return factor_of


def bell_draw(own_key, extent, width, limit, pieces=(), held_as=jnp.bfloat16):
    loudness = block_scale(own_key, extent, pieces, -0.22, 0.18) if pieces else 1.0
    values = jax.random.normal(own_key, extent, jnp.float32) * width * loudness
    return jnp.minimum(jnp.maximum(values, -limit), limit).astype(held_as)


def bell_draw_with(stream_key, shape, scale, bound, shards, heavy, held_as=jnp.bfloat16):
    drawn = scale * jax.random.normal(stream_key, shape, jnp.float32)
    if shards:
        drawn = drawn * block_scale(stream_key, shape, shards, -0.22, 0.18)
    return jnp.clip(strengthened(drawn, jax.random.fold_in(stream_key, 3), *heavy), -bound, bound).astype(held_as)


def setup_inputs(seed: int = 0) -> dict:
    keys = jax.random.split(jax.random.key(seed), 8)
    members = bell_draw_with(keys[0], (MEMBERS, LEV, P_SIZE), 1.0, 6.0, ((0, 32), (1, 8)), (0, 2, 32, 2.75))
    direction = draw_direction(jax.random.fold_in(keys[7], 71), 0)
    residual = draw_residual(jax.random.fold_in(keys[7], 71), 0)
    iterate = bell_draw(keys[3], (LEV, P_SIZE), 1.0, 6.0, ((0, 8), (1, 32)), jnp.float32)
    tiles = bell_draw(keys[4], (NB, BR, TILE, TILE), (BR * TILE) ** -0.5, 0.25)
    columns = draw_columns(jax.random.fold_in(keys[7], 71), 0)
    vertical = bell_draw(keys[6], (LEV, 2 * REACH + 1), (2 * REACH + 1) ** -0.5, 2.0, (), jnp.float32)
    return dict(members=members, direction=direction, residual=residual, iterate=iterate, tiles=tiles, columns=columns, vertical=vertical)


def adjoint_levels(field, band):
    count = field.shape[0]
    rimmed = jnp.pad(field.astype(jnp.float32), ((REACH, REACH), (0, 0)))
    padded_band = jnp.pad(band, ((REACH, REACH), (0, 0)))
    result = jnp.zeros(field.shape, jnp.float32)
    for offset in range(2 * REACH + 1):
        start = 2 * REACH - offset
        result = result + padded_band[start:start + count, offset][:, None] * rimmed[start:start + count]
    return result


def forward_levels(field, band):
    count = field.shape[0]
    rimmed = jnp.pad(field.astype(jnp.float32), ((REACH, REACH), (0, 0)))
    result = jnp.zeros(field.shape, jnp.float32)
    for offset in range(2 * REACH + 1):
        result = result + band[:, offset][:, None] * rimmed[offset:offset + count]
    return result


def member_term(member, direction, tiles, columns, vertical):
    levels, points = member.shape
    blocks, per_row, tile = tiles.shape[0], tiles.shape[1], tiles.shape[2]
    wide_tiles = tiles.astype(jnp.float32)
    mixed = (member.astype(jnp.float32) * direction).astype(jnp.bfloat16).reshape(levels, blocks, tile)
    spread = jnp.einsum("vra,rjab->rjvb", mixed.astype(jnp.float32), wide_tiles, precision=lax.Precision.HIGHEST)
    onehot = (columns[None, :, :] == jnp.arange(blocks, dtype=jnp.int32)[:, None, None]).astype(jnp.float32)
    back = jnp.einsum("crj,rjvb->vcb", onehot, spread, precision=lax.Precision.HIGHEST)
    back = back.astype(jnp.bfloat16).reshape(levels, points)
    lifted = adjoint_levels(back, vertical).astype(jnp.bfloat16).reshape(levels, blocks, tile)
    picked = lifted[:, columns]
    forward = jnp.einsum("vrjb,rjab->vra", picked.astype(jnp.float32), wide_tiles, precision=lax.Precision.HIGHEST)
    forward = forward.astype(jnp.bfloat16).reshape(levels, points)
    return member.astype(jnp.float32) * forward_levels(forward, vertical)


def reference(members, direction, residual, iterate, tiles, columns, vertical):
    def accumulate(running, member):
        return running + member_term(member, direction, tiles, columns, vertical), None

    total, unused = lax.scan(accumulate, jnp.zeros(direction.shape, jnp.float32), members)
    image = direction + total / (members.shape[0] - 1)
    norm_old = jnp.sum(residual * residual)
    curvature = jnp.sum(direction * image)
    alpha = norm_old / curvature
    iterate_new = iterate + alpha * direction
    residual_new = residual - alpha * image
    norm_new = jnp.sum(residual_new * residual_new)
    direction_new = residual_new + (norm_new / norm_old) * direction
    return iterate_new, residual_new, direction_new
```

```python
import jax
import jax.numpy as jnp
from jax import lax
from jax.experimental import pallas as pl
from jax.experimental.pallas import tpu as pltpu
from jax.sharding import PartitionSpec as P

REACH = 4
HALO = 2 * REACH
CHUNKS = 16
F32 = jnp.float32
BF16 = jnp.bfloat16
NT = (((1,), (1,)), ((), ()))


def split3(value):
    high = value.astype(BF16)
    rest = value - high.astype(F32)
    middle = rest.astype(BF16)
    low = (rest - middle.astype(F32)).astype(BF16)
    return jnp.concatenate([high, middle, low], axis=0)


def product_kernel(
    columns_ref, band_ref, members_ref, direction_ref, below_ref, above_ref, tiles_hbm,
    out_ref, tiles_ref, smooth_ref, acc_ref, back_ref, sems,
):
    mem_dev, lev_dev, points = members_ref.shape
    blocks, per_row, tile, _ = tiles_ref.shape
    vectors = mem_dev * lev_dev
    part = blocks // CHUNKS

    def fetch(i):
        rows = pl.ds(i * part, part)
        return pltpu.make_async_copy(tiles_hbm.at[rows], tiles_ref.at[rows], sems.at[i])

    for i in range(CHUNKS):
        fetch(i).start()

    band = split3(band_ref[...])
    acc_ref[...] = jnp.zeros_like(acc_ref)

    def vertical_step(g, carry):
        cols = pl.ds(pl.multiple_of(g * 2 * tile, 2 * tile), 2 * tile)
        field = direction_ref[:, cols]
        mixed = [(members_ref[m, :, cols].astype(F32) * field).astype(BF16) for m in range(mem_dev)]
        stacked = jnp.concatenate(mixed + [below_ref[:, cols], above_ref[:, cols]], axis=0)
        three = jnp.dot(band, stacked, preferred_element_type=F32)
        total = (three[2 * vectors :] + three[vectors : 2 * vectors]) + three[:vectors]
        total = total.astype(BF16)
        smooth_ref[2 * g] = total[:, :tile]
        smooth_ref[2 * g + 1] = total[:, tile:]
        return carry

    lax.fori_loop(0, blocks // 2, vertical_step, 0, unroll=2)

    def adjoint_step(r, carry):
        left = smooth_ref[r]
        where = [columns_ref[r * per_row + j] for j in range(per_row)]
        old = [acc_ref[c] for c in where]
        new = [
            old[j] + jnp.dot(left, tiles_ref[r, j], preferred_element_type=F32)
            for j in range(per_row)
        ]
        for j in range(per_row):
            acc_ref[where[j]] = new[j]
        return carry

    for i in range(CHUNKS):
        fetch(i).wait()
        lax.fori_loop(i * part, (i + 1) * part, adjoint_step, 0, unroll=4)

    back_ref[...] = acc_ref[...].astype(BF16)

    def forward_row(r):
        left = jnp.concatenate(
            [back_ref[columns_ref[r * per_row + j]] for j in range(per_row)], axis=1
        )
        right = jnp.concatenate([tiles_ref[r, j] for j in range(per_row)], axis=1)
        field = lax.dot_general(left, right, NT, preferred_element_type=F32)
        cols = pl.ds(pl.multiple_of(r * tile, tile), tile)
        total = jnp.zeros((lev_dev, tile), F32)
        for m in range(mem_dev):
            total = total + members_ref[m, :, cols].astype(F32) * field[m * lev_dev : (m + 1) * lev_dev]
        return total

    wide = out_ref.shape[2] // tile

    def forward_step(g, carry):
        for k in range(wide):
            out_ref[g, :, k * tile : (k + 1) * tile] = forward_row(g * wide + k).astype(out_ref.dtype)
        return carry

    lax.fori_loop(0, blocks // wide, forward_step, 0, unroll=2)


def two_sum(a, b):
    s = a + b
    t = s - a
    return s, (a - (s - t)) + (b - t)


def two_product(a, b):
    def halves(x):
        t = 4097.0 * x
        high = t - (t - x)
        return high, x - high

    p = a * b
    ah, al = halves(a)
    bh, bl = halves(b)
    return p, ((ah * bh - p) + ah * bl + al * bh) + al * bl


def add_pairs(a, b):
    s, e = two_sum(a[0], b[0])
    return two_sum(s, e + (a[1] + b[1]))


def sum_pairs(pairs):
    while len(pairs) > 1:
        rest = pairs[len(pairs) // 2 * 2 :]
        pairs = [add_pairs(pairs[i], pairs[i + 1]) for i in range(0, len(pairs) - 1, 2)] + rest
    return pairs[0]


def rows_of(pair):
    return [(pair[0][i : i + 1], pair[1][i : i + 1]) for i in range(pair[0].shape[0])]


def dot_pairs(a, b):
    pair = two_product(a, b)
    lanes = a.shape[1]
    pieces = [
        (pair[0][i : i + 8, j : j + 128], pair[1][i : i + 8, j : j + 128])
        for i in range(0, a.shape[0], 8)
        for j in range(0, lanes, 128)
    ]
    return sum_pairs(rows_of(sum_pairs(pieces)))


def image_kernel(share_ref, parts_ref, direction_ref, residual_ref, image_ref, sums_ref, *, scale):
    total = parts_ref[0].astype(F32)
    for i in range(1, parts_ref.shape[0]):
        total = total + parts_ref[i].astype(F32)
    own = direction_ref[...]
    residual = residual_ref[...]
    image = own + total / scale
    image_ref[...] = image
    rr = dot_pairs(residual, residual)
    ri = dot_pairs(residual, image)
    ii = dot_pairs(image, image)
    di = dot_pairs(own, image)
    sums_ref[...] = jnp.concatenate([rr[0], rr[1], ri[0], ri[1], ii[0], ii[1], di[0], di[1]], axis=0)


def add_devices(parts_ref):
    pairs = []
    for k in range(4):
        pairs.append(
            sum_pairs(
                [(parts_ref[i, 2 * k : 2 * k + 1], parts_ref[i, 2 * k + 1 : 2 * k + 2]) for i in range(parts_ref.shape[0])]
            )
        )
    return pairs


def gather_kernel(parts_ref, out_ref):
    out_ref[...] = jnp.concatenate([x for pair in add_devices(parts_ref) for x in pair], axis=0)


def update_kernel(share_ref, parts_ref, direction_ref, residual_ref, iterate_ref, image_ref, x_ref, r_ref, d_ref):
    pairs = add_devices(parts_ref)
    lanes = 128
    while lanes > 1:
        lanes //= 2
        pairs = [add_pairs((h[:, :lanes], l[:, :lanes]), (h[:, lanes:], l[:, lanes:])) for h, l in pairs]
    rr, ri, ii, di = pairs
    norm_old = rr[0] + rr[1]
    alpha = norm_old / (di[0] + di[1])

    def scaled(pair):
        p, e = two_product(pair[0], alpha)
        return p, e + pair[1] * alpha

    inner = add_pairs(scaled(ii), (-2.0 * ri[0], -2.0 * ri[1]))
    norm_new = add_pairs(rr, scaled(inner))
    beta = (norm_new[0] + norm_new[1]) / norm_old
    own = direction_ref[...]
    residual_new = residual_ref[...] - alpha * image_ref[...]
    x_ref[...] = iterate_ref[...] + alpha * own
    r_ref[...] = residual_new
    d_ref[...] = residual_new + beta * own


def gathered(value, axis):
    count = lax.axis_size(axis)
    return lax.all_to_all(
        jnp.broadcast_to(value[None], (count,) + value.shape), axis, 0, 0, tiled=True
    )


def level_matrix(vertical, level_start, lev_dev, mem_dev):
    levels = vertical.shape[0]
    span = lev_dev + 2 * HALO
    padded = jnp.pad(vertical, ((HALO, HALO), (0, 0)))
    band = lax.dynamic_slice_in_dim(padded, level_start, span, 0)
    width = span + 2 * REACH
    row = lax.broadcasted_iota(jnp.int32, (span, width), 0)
    col = lax.broadcasted_iota(jnp.int32, (span, width), 1)
    level = col + (level_start - HALO - REACH)
    dense = jnp.zeros((span, width), F32)
    for offset in range(2 * REACH + 1):
        dense = jnp.where(col == row + offset, band[:, offset : offset + 1], dense)
    dense = jnp.where((level >= 0) & (level < levels), dense, 0.0)
    both = jnp.einsum("lq,kq->lk", dense[HALO : HALO + lev_dev], dense, precision=lax.Precision.HIGHEST)
    own, low, high = both[:, HALO : HALO + lev_dev], both[:, :HALO], both[:, HALO + lev_dev :]
    eye = jnp.eye(mem_dev, dtype=F32)
    return jnp.concatenate([jnp.kron(eye, own), jnp.kron(eye, low), jnp.kron(eye, high)], axis=1)


def on_device(members, direction, residual, iterate, tiles, columns, vertical):
    mem_dev, lev_dev, points = members.shape
    blocks, per_row, tile = tiles.shape[:3]
    vectors = mem_dev * lev_dev
    groups = lax.axis_size("member")
    share = points // groups
    slabs = lax.axis_size("slab")
    member_count = mem_dev * groups
    level_start = lax.axis_index("slab") * lev_dev

    def edge(start):
        mixed = members[:, start : start + HALO].astype(F32) * direction[None, start : start + HALO]
        return mixed.astype(BF16).reshape(mem_dev * HALO, points)

    upward = [(i, i + 1) for i in range(slabs - 1)]
    downward = [(target, source) for source, target in upward]
    below = lax.ppermute(edge(lev_dev - HALO), "slab", upward)
    above = lax.ppermute(edge(0), "slab", downward)
    band = level_matrix(vertical, level_start, lev_dev, mem_dev)

    vmem = pl.BlockSpec(memory_space=pltpu.VMEM)
    smem = pl.BlockSpec(memory_space=pltpu.SMEM)
    partial_value = pl.pallas_call(
        product_kernel,
        out_shape=jax.ShapeDtypeStruct((groups, lev_dev, share), BF16),
        in_specs=[smem, vmem, vmem, vmem, vmem, vmem, pl.BlockSpec(memory_space=pl.ANY)],
        out_specs=vmem,
        scratch_shapes=[
            pltpu.VMEM(tiles.shape, BF16),
            pltpu.VMEM((blocks, vectors, tile), BF16),
            pltpu.VMEM((blocks, vectors, tile), F32),
            pltpu.VMEM((blocks, vectors, tile), BF16),
            pltpu.SemaphoreType.DMA((CHUNKS,)),
        ],
        compiler_params=pltpu.CompilerParams(vmem_limit_bytes=40 * 2**20),
        name="product",
    )(columns.reshape(-1), band, members, direction, below, above, tiles)

    parts = lax.all_to_all(partial_value, "member", 0, 0, tiled=True)
    me = lax.axis_index("member").reshape(1)
    whole = lambda shape: pl.BlockSpec(shape, lambda i, s: (0,) * len(shape))
    own = pl.BlockSpec((lev_dev, share), lambda i, s: (0, s[0]))
    field = jax.ShapeDtypeStruct((lev_dev, share), F32)
    square = whole((lev_dev, share))
    image, sums = pl.pallas_call(
        lambda *refs: image_kernel(*refs, scale=float(member_count - 1)),
        out_shape=(field, jax.ShapeDtypeStruct((8, 128), F32)),
        grid_spec=pltpu.PrefetchScalarGridSpec(
            num_scalar_prefetch=1,
            grid=(1,),
            in_specs=[whole((groups, lev_dev, share)), own, square],
            out_specs=(square, whole((8, 128))),
        ),
        name="image",
    )(me, parts, direction, residual)

    first = gathered(sums, "slab")
    middle = pl.pallas_call(
        gather_kernel, out_shape=jax.ShapeDtypeStruct((8, 128), F32), in_specs=[vmem], out_specs=vmem, name="gather"
    )(first)
    second = gathered(middle, "member")
    return pl.pallas_call(
        update_kernel,
        out_shape=(field, field, field),
        grid_spec=pltpu.PrefetchScalarGridSpec(
            num_scalar_prefetch=1,
            grid=(1,),
            in_specs=[whole((groups, 8, 128)), own, square, square, square],
            out_specs=(square, square, square),
        ),
        name="update",
    )(me, second, direction, residual, iterate, image)


def solution(mesh):
    placed = (
        P("member", "slab", None),
        P("slab", None),
        P("slab", "member"),
        P("slab", "member"),
        P(),
        P(),
        P(),
    )
    return jax.shard_map(
        on_device,
        mesh=mesh,
        in_specs=placed,
        out_specs=(P("slab", "member"), P("slab", "member"), P("slab", "member")),
        check_vma=False,
    )
```

```python
import functools

import jax
import jax.numpy as jnp
from jax import lax
from jax.experimental import pallas as pl
from jax.experimental.pallas import tpu as pltpu
from jax.sharding import PartitionSpec as P

REACH = 4
HALO = 2 * REACH
EDGE_CHUNKS = 4
TILE_CHUNKS = 8
F32 = jnp.float32
BF16 = jnp.bfloat16
NT = (((1,), (1,)), ((), ()))
VMEM = pl.BlockSpec(memory_space=pltpu.VMEM)
HBM = pl.BlockSpec(memory_space=pltpu.HBM)


def edge_kernel(members_hbm, direction_hbm, low_ref, high_ref, members_ref, direction_ref, sems):
    mem_dev, lev_dev, points = members_ref.shape
    step = points // EDGE_CHUNKS

    def copies(i):
        cols = pl.ds(i * step, step)
        return (
            pltpu.make_async_copy(direction_hbm.at[:, cols], direction_ref.at[:, cols], sems.at[2 * i]),
            pltpu.make_async_copy(members_hbm.at[:, :, cols], members_ref.at[:, :, cols], sems.at[2 * i + 1]),
        )

    for i in range(EDGE_CHUNKS):
        for copy in copies(i):
            copy.start()
    for i in range(EDGE_CHUNKS):
        for copy in copies(i):
            copy.wait()
        cols = slice(i * step, (i + 1) * step)
        low, high = [], []
        for m in range(mem_dev):
            low.append(members_ref[m, : 2 * HALO, cols].astype(F32)[:HALO] * direction_ref[:HALO, cols])
            high.append(members_ref[m, lev_dev - 2 * HALO :, cols].astype(F32)[HALO:] * direction_ref[lev_dev - HALO :, cols])
        low_ref[:, cols] = jnp.concatenate(low, axis=0).astype(BF16)
        high_ref[:, cols] = jnp.concatenate(high, axis=0).astype(BF16)


def split3(value):
    high = value.astype(BF16)
    rest = value - high.astype(F32)
    middle = rest.astype(BF16)
    low = (rest - middle.astype(F32)).astype(BF16)
    return jnp.concatenate([high, middle, low], axis=0)


def level_matrix(band, level_start, levels, lev_dev, mem_dev):
    span = band.shape[0]
    lanes = 128
    row = lax.broadcasted_iota(jnp.int32, (span, lanes), 0)
    col = lax.broadcasted_iota(jnp.int32, (span, lanes), 1)
    dense = jnp.zeros((span, lanes), F32)
    for offset in range(2 * REACH + 1):
        dense = jnp.where(col == row + offset, band[:, offset : offset + 1], dense)
    level = col + (level_start - HALO - REACH)
    dense = jnp.where((level >= 0) & (level < levels), dense, 0.0)
    own, low, high = dense[HALO : HALO + lev_dev], dense[:HALO], dense[HALO + lev_dev :]
    rows = jnp.concatenate([own] * mem_dev, axis=0)
    cols = jnp.concatenate([own] * mem_dev + [low] * mem_dev + [high] * mem_dev, axis=0)
    both = lax.dot_general(rows, cols, NT, precision=lax.Precision.HIGHEST, preferred_element_type=F32)
    i = lax.broadcasted_iota(jnp.int32, both.shape, 0)
    j = lax.broadcasted_iota(jnp.int32, both.shape, 1)
    keep = jnp.zeros(both.shape, jnp.bool_)
    vectors = mem_dev * lev_dev
    for m in range(mem_dev):
        mine = (i >= m * lev_dev) & (i < (m + 1) * lev_dev)
        theirs = (j >= m * lev_dev) & (j < (m + 1) * lev_dev)
        for first in (vectors + m * HALO, vectors + (mem_dev + m) * HALO):
            theirs = theirs | ((j >= first) & (j < first + HALO))
        keep = keep | (mine & theirs)
    return jnp.where(keep, both, 0.0)


def stage_kernel(
    vertical_ref, direction_ref, tiles_hbm, residual_hbm, iterate_hbm,
    tiles_ref, residual_ref, iterate_ref, own_ref, band_ref, padded_ref, sems,
    *, mem_dev,
):
    copies = [
        pltpu.make_async_copy(residual_hbm, residual_ref, sems.at[0]),
        pltpu.make_async_copy(iterate_hbm, iterate_ref, sems.at[1]),
    ]
    part = tiles_ref.shape[0] // TILE_CHUNKS
    for i in range(TILE_CHUNKS):
        rows = pl.ds(i * part, part)
        copies.append(pltpu.make_async_copy(tiles_hbm.at[rows], tiles_ref.at[rows], sems.at[2 + i]))
    for copy in copies:
        copy.start()
    lev_dev, share = own_ref.shape
    levels, width = vertical_ref.shape
    level_start = lax.axis_index("slab") * lev_dev
    own_ref[...] = direction_ref[:, pl.ds(pl.multiple_of(lax.axis_index("member") * share, share), share)]
    padded_ref[...] = jnp.zeros_like(padded_ref)
    padded_ref[HALO : HALO + levels, :width] = vertical_ref[...]
    band = padded_ref[pl.ds(pl.multiple_of(level_start, lev_dev), lev_dev + 2 * HALO), :]
    band_ref[...] = split3(level_matrix(band, level_start, levels, lev_dev, mem_dev))
    for copy in copies:
        copy.wait()


def product_kernel(
    columns_hbm, band_ref, members_ref, direction_ref, below_ref, above_ref, tiles_ref,
    out_ref, columns_ref, smooth_ref, acc_ref, back_ref, sem,
):
    mem_dev, lev_dev, points = members_ref.shape
    blocks, per_row, tile, _ = tiles_ref.shape
    vectors = mem_dev * lev_dev
    fetch = pltpu.make_async_copy(columns_hbm, columns_ref, sem)
    fetch.start()
    band = band_ref[...]
    acc_ref[...] = jnp.zeros_like(acc_ref)

    def vertical_step(g, carry):
        cols = pl.ds(pl.multiple_of(g * 2 * tile, 2 * tile), 2 * tile)
        field = direction_ref[:, cols]
        mixed = [(members_ref[m, :, cols].astype(F32) * field).astype(BF16) for m in range(mem_dev)]
        stacked = jnp.concatenate(mixed + [below_ref[:, cols], above_ref[:, cols]], axis=0)
        three = jnp.dot(band, stacked, preferred_element_type=F32)
        total = (three[2 * vectors :] + three[vectors : 2 * vectors]) + three[:vectors]
        total = total.astype(BF16)
        smooth_ref[2 * g] = total[:, :tile]
        smooth_ref[2 * g + 1] = total[:, tile:]
        return carry

    lax.fori_loop(0, blocks // 2, vertical_step, 0, unroll=8)
    fetch.wait()

    def adjoint_step(r, carry):
        left = smooth_ref[r]
        where = [columns_ref[r, j] for j in range(per_row)]
        right = jnp.concatenate([tiles_ref[r, j] for j in range(per_row)], axis=1)
        spread = jnp.dot(left, right, preferred_element_type=F32)
        new = [acc_ref[where[j]] + spread[:, j * tile : (j + 1) * tile] for j in range(per_row)]
        for j in range(per_row):
            acc_ref[where[j]] = new[j]
        return carry

    lax.fori_loop(0, blocks, adjoint_step, 0, unroll=4)
    back_ref[...] = acc_ref[...].astype(BF16)

    def forward_row(r):
        left = jnp.concatenate([back_ref[columns_ref[r, j]] for j in range(per_row)], axis=1)
        right = jnp.concatenate([tiles_ref[r, j] for j in range(per_row)], axis=1)
        field = lax.dot_general(left, right, NT, preferred_element_type=F32)
        cols = pl.ds(pl.multiple_of(r * tile, tile), tile)
        total = members_ref[0, :, cols].astype(F32) * field[:lev_dev]
        for m in range(1, mem_dev):
            total = total + members_ref[m, :, cols].astype(F32) * field[m * lev_dev : (m + 1) * lev_dev]
        return total

    wide = out_ref.shape[2] // tile

    def forward_step(g, carry):
        for k in range(wide):
            out_ref[g, :, k * tile : (k + 1) * tile] = forward_row(g * wide + k).astype(out_ref.dtype)
        return carry

    lax.fori_loop(0, blocks // wide, forward_step, 0, unroll=8)


def full_sum(value):
    return jnp.sum(jnp.sum(value, axis=0, keepdims=True), axis=1, keepdims=True)


def image_kernel(parts_ref, own_ref, residual_ref, image_ref, sums_ref, *, scale):
    total = parts_ref[0].astype(F32)
    for i in range(1, parts_ref.shape[0]):
        total = total + parts_ref[i].astype(F32)
    own = own_ref[...]
    residual = residual_ref[...]
    image = own + total / scale
    image_ref[...] = image
    rr = full_sum(residual * residual)
    di = full_sum(own * image)
    ii = full_sum(image * image)
    ri = full_sum(residual * image)
    guess = jnp.where(ii > 0.0, ri / jnp.where(ii > 0.0, ii, 1.0), 0.0)
    left = residual - guess * image
    ll = full_sum(left * left)
    li = full_sum(left * image)
    lane = lax.broadcasted_iota(jnp.int32, (1, sums_ref.shape[1]), 1)
    row = jnp.zeros(lane.shape, F32)
    for k, value in enumerate((rr, di, ll, li, ii, guess)):
        row = jnp.where(lane == k, value, row)
    sums_ref[...] = jnp.broadcast_to(row, sums_ref.shape)


def update_kernel(parts_ref, own_ref, residual_ref, iterate_ref, image_ref, x_ref, r_ref, d_ref):
    parts = parts_ref[...]
    sums = jnp.sum(parts, axis=0, keepdims=True)
    norm_old = sums[:, 0:1]
    alpha = norm_old / sums[:, 1:2]
    ll, li, ii, guess = (parts[:, k : k + 1] for k in range(2, 6))
    shift = guess - alpha
    norm_new = jnp.sum(ll + shift * (2.0 * li + shift * ii), axis=0, keepdims=True)
    own = own_ref[...]
    residual_new = residual_ref[...] - alpha * image_ref[...]
    x_ref[...] = iterate_ref[...] + alpha * own
    r_ref[...] = residual_new
    d_ref[...] = residual_new + (norm_new / norm_old) * own


def on_device(members, direction, residual, iterate, tiles, columns, vertical):
    mem_dev, lev_dev, points = members.shape
    blocks, per_row, tile = tiles.shape[:3]
    vectors = mem_dev * lev_dev
    groups, slabs = lax.axis_size("member"), lax.axis_size("slab")
    share = points // groups
    member_count = mem_dev * groups
    levels, width = vertical.shape
    square = (lev_dev, share)
    edge = (mem_dev * HALO, points)

    far = functools.partial(pltpu.with_memory_space_constraint, memory_space=pltpu.HBM)
    low, high, members_near, direction_near = pl.pallas_call(
        edge_kernel,
        out_shape=(
            pltpu.VMEM(edge, BF16), pltpu.VMEM(edge, BF16),
            pltpu.VMEM(members.shape, BF16), pltpu.VMEM(direction.shape, F32),
        ),
        in_specs=[HBM, HBM],
        out_specs=(VMEM,) * 4,
        scratch_shapes=[pltpu.SemaphoreType.DMA((2 * EDGE_CHUNKS,))],
        compiler_params=pltpu.CompilerParams(vmem_limit_bytes=32 * 2**20),
        name="edge",
    )(far(members), far(direction))
    below = lax.ppermute(high, "slab", [(i, (i + 1) % slabs) for i in range(slabs)])
    above = lax.ppermute(low, "slab", [((i + 1) % slabs, i) for i in range(slabs)])

    tiles_near, residual_near, iterate_near, own, band = pl.pallas_call(
        functools.partial(stage_kernel, mem_dev=mem_dev),
        out_shape=(
            pltpu.VMEM(tiles.shape, BF16), pltpu.VMEM(square, F32), pltpu.VMEM(square, F32), pltpu.VMEM(square, F32),
            pltpu.VMEM((3 * vectors, vectors + 2 * mem_dev * HALO), BF16),
        ),
        in_specs=[VMEM, VMEM, HBM, HBM, HBM],
        out_specs=(VMEM,) * 5,
        scratch_shapes=[
            pltpu.VMEM((levels + 2 * HALO, 128), F32),
            pltpu.SemaphoreType.DMA((2 + TILE_CHUNKS,)),
        ],
        compiler_params=pltpu.CompilerParams(vmem_limit_bytes=32 * 2**20),
        cost_estimate=pl.CostEstimate(flops=0, bytes_accessed=2 * tiles.size * 2, transcendentals=0),
        name="stage",
    )(vertical, direction_near, far(tiles), far(residual), far(iterate))

    partial_value = pl.pallas_call(
        product_kernel,
        out_shape=pltpu.VMEM((groups, lev_dev, share), BF16),
        in_specs=[HBM] + [VMEM] * 6,
        out_specs=VMEM,
        scratch_shapes=[
            pltpu.SMEM((blocks, per_row), jnp.int32),
            pltpu.VMEM((blocks, vectors, tile), BF16),
            pltpu.VMEM((blocks, vectors, tile), F32),
            pltpu.VMEM((blocks, vectors, tile), BF16),
            pltpu.SemaphoreType.DMA,
        ],
        compiler_params=pltpu.CompilerParams(vmem_limit_bytes=32 * 2**20),
        name="product",
    )(far(columns), band, members_near, direction_near, below, above, tiles_near)

    parts = lax.all_to_all(partial_value, "member", 0, 0, tiled=True)
    devices = groups * slabs
    image, sums = pl.pallas_call(
        functools.partial(image_kernel, scale=float(member_count - 1)),
        out_shape=(pltpu.VMEM(square, F32), pltpu.VMEM((devices, 128), F32)),
        in_specs=[VMEM] * 3,
        out_specs=(VMEM,) * 2,
        name="image",
    )(parts, own, residual_near)

    spread = lax.all_to_all(sums.reshape(devices, 1, 128), ("member", "slab"), 0, 0, tiled=True)
    field = jax.ShapeDtypeStruct(square, F32)
    return pl.pallas_call(
        update_kernel,
        out_shape=(field, field, field),
        in_specs=[VMEM] * 5,
        out_specs=(VMEM,) * 3,
        name="update",
    )(spread.reshape(devices, 128), own, residual_near, iterate_near, image)


def solution(mesh):
    placed = (
        P("member", "slab", None),
        P("slab", None),
        P("slab", "member"),
        P("slab", "member"),
        P(),
        P(),
        P(),
    )
    return jax.shard_map(
        on_device,
        mesh=mesh,
        in_specs=placed,
        out_specs=(P("slab", "member"), P("slab", "member"), P("slab", "member")),
        check_vma=False,
    )
```

```python
import functools

import jax
import jax.numpy as jnp
from jax import lax
from jax.experimental import pallas as pl
from jax.experimental.pallas import tpu as pltpu
from jax.sharding import PartitionSpec as P

REACH = 4
HALO = 2 * REACH
EDGE_CHUNKS = 4
TILE_CHUNKS = 8
LANES = 128
F32 = jnp.float32
BF16 = jnp.bfloat16
NT = (((1,), (1,)), ((), ()))
VMEM = pl.BlockSpec(memory_space=pltpu.VMEM)
HBM = pl.BlockSpec(memory_space=pltpu.HBM)


def edge_kernel(members_hbm, direction_hbm, low_ref, high_ref, members_ref, rim_ref, sems):
    mem_dev, lev_dev, points = members_ref.shape
    step = points // EDGE_CHUNKS

    def copies(i):
        cols = pl.ds(i * step, step)
        last = pl.ds(lev_dev - HALO, HALO)
        return (
            pltpu.make_async_copy(direction_hbm.at[pl.ds(0, HALO), cols], rim_ref.at[0, :, cols], sems.at[3 * i]),
            pltpu.make_async_copy(direction_hbm.at[last, cols], rim_ref.at[1, :, cols], sems.at[3 * i + 1]),
            pltpu.make_async_copy(members_hbm.at[:, :, cols], members_ref.at[:, :, cols], sems.at[3 * i + 2]),
        )

    for i in range(EDGE_CHUNKS):
        for copy in copies(i):
            copy.start()
    for i in range(EDGE_CHUNKS):
        for copy in copies(i):
            copy.wait()
        cols = slice(i * step, (i + 1) * step)
        low, high = [], []
        for m in range(mem_dev):
            low.append(members_ref[m, : 2 * HALO, cols].astype(F32)[:HALO] * rim_ref[0, :, cols])
            high.append(members_ref[m, lev_dev - 2 * HALO :, cols].astype(F32)[HALO:] * rim_ref[1, :, cols])
        low_ref[:, cols] = jnp.concatenate(low, axis=0).astype(BF16)
        high_ref[:, cols] = jnp.concatenate(high, axis=0).astype(BF16)


def split3(value):
    high = value.astype(BF16)
    rest = value - high.astype(F32)
    middle = rest.astype(BF16)
    low = (rest - middle.astype(F32)).astype(BF16)
    return jnp.concatenate([high, middle, low], axis=0)


def level_matrix(band, level_start, levels, lev_dev, mem_dev):
    span = band.shape[0]
    lanes = 128
    row = lax.broadcasted_iota(jnp.int32, (span, lanes), 0)
    col = lax.broadcasted_iota(jnp.int32, (span, lanes), 1)
    dense = jnp.zeros((span, lanes), F32)
    for offset in range(2 * REACH + 1):
        dense = jnp.where(col == row + offset, band[:, offset : offset + 1], dense)
    level = col + (level_start - HALO - REACH)
    dense = jnp.where((level >= 0) & (level < levels), dense, 0.0)
    own, low, high = dense[HALO : HALO + lev_dev], dense[:HALO], dense[HALO + lev_dev :]
    rows = jnp.concatenate([own] * mem_dev, axis=0)
    cols = jnp.concatenate([own] * mem_dev + [low] * mem_dev + [high] * mem_dev, axis=0)
    both = lax.dot_general(rows, cols, NT, precision=lax.Precision.HIGHEST, preferred_element_type=F32)
    i = lax.broadcasted_iota(jnp.int32, both.shape, 0)
    j = lax.broadcasted_iota(jnp.int32, both.shape, 1)
    keep = jnp.zeros(both.shape, jnp.bool_)
    vectors = mem_dev * lev_dev
    for m in range(mem_dev):
        mine = (i >= m * lev_dev) & (i < (m + 1) * lev_dev)
        theirs = (j >= m * lev_dev) & (j < (m + 1) * lev_dev)
        for first in (vectors + m * HALO, vectors + (mem_dev + m) * HALO):
            theirs = theirs | ((j >= first) & (j < first + HALO))
        keep = keep | (mine & theirs)
    return jnp.where(keep, both, 0.0)


def stage_kernel(
    vertical_ref, direction_hbm, tiles_hbm, residual_hbm, iterate_hbm,
    tiles_ref, direction_ref, residual_ref, iterate_ref, own_ref, band_ref, padded_ref, sems,
    *, mem_dev,
):
    lev_dev, share = own_ref.shape
    mine = pl.ds(pl.multiple_of(lax.axis_index("member") * share, share), share)
    copies = [
        pltpu.make_async_copy(direction_hbm, direction_ref, sems.at[0]),
        pltpu.make_async_copy(direction_hbm.at[:, mine], own_ref, sems.at[1]),
        pltpu.make_async_copy(residual_hbm, residual_ref, sems.at[2]),
        pltpu.make_async_copy(iterate_hbm, iterate_ref, sems.at[3]),
    ]
    part = tiles_ref.shape[0] // TILE_CHUNKS
    for i in range(TILE_CHUNKS):
        rows = pl.ds(i * part, part)
        copies.append(pltpu.make_async_copy(tiles_hbm.at[rows], tiles_ref.at[rows], sems.at[4 + i]))
    for copy in copies:
        copy.start()
    width, levels = vertical_ref.shape
    level_start = lax.axis_index("slab") * lev_dev
    padded_ref[...] = jnp.zeros_like(padded_ref)
    padded_ref[:width, LANES : LANES + levels] = vertical_ref[...]
    total = padded_ref.shape[1]
    turned = pltpu.roll(padded_ref[...], total - (LANES - HALO + level_start), 1)[:, :LANES]
    band = jnp.concatenate([turned, jnp.zeros((LANES - turned.shape[0], LANES), F32)], axis=0).T
    band_ref[...] = split3(level_matrix(band[: lev_dev + 2 * HALO], level_start, levels, lev_dev, mem_dev))
    for copy in copies:
        copy.wait()


def product_kernel(
    columns_hbm, band_ref, members_ref, direction_ref, below_ref, above_ref, tiles_ref,
    out_ref, columns_ref, smooth_ref, acc_ref, back_ref, sem,
):
    mem_dev, lev_dev, points = members_ref.shape
    blocks, per_row, tile, _ = tiles_ref.shape
    vectors = mem_dev * lev_dev
    fetch = pltpu.make_async_copy(columns_hbm, columns_ref, sem)
    fetch.start()
    band = band_ref[...]

    def vertical_step(g, carry):
        cols = pl.ds(pl.multiple_of(g * 2 * tile, 2 * tile), 2 * tile)
        field = direction_ref[:, cols]
        mixed = [(members_ref[m, :, cols].astype(F32) * field).astype(BF16) for m in range(mem_dev)]
        stacked = jnp.concatenate(mixed + [below_ref[:, cols], above_ref[:, cols]], axis=0)
        three = jnp.dot(band, stacked, preferred_element_type=F32)
        total = (three[2 * vectors :] + three[vectors : 2 * vectors]) + three[:vectors]
        total = total.astype(BF16)
        smooth_ref[2 * g] = total[:, :tile]
        smooth_ref[2 * g + 1] = total[:, tile:]
        for k in range(2):
            acc_ref[2 * g + k] = jnp.zeros((vectors, tile), F32)
        return carry

    lax.fori_loop(0, blocks // 2, vertical_step, 0, unroll=16)
    fetch.wait()

    def adjoint_step(r, carry):
        left = smooth_ref[r]
        where = [columns_ref[j, r] for j in range(per_row)]
        right = jnp.concatenate([tiles_ref[r, j] for j in range(per_row)], axis=1)
        spread = jnp.dot(left, right, preferred_element_type=F32)
        new = [acc_ref[where[j]] + spread[:, j * tile : (j + 1) * tile] for j in range(per_row)]
        for j in range(per_row):
            acc_ref[where[j]] = new[j]
        return carry

    lax.fori_loop(0, blocks, adjoint_step, 0, unroll=16)
    back_ref[...] = acc_ref[...].astype(BF16)

    def forward_row(r):
        left = jnp.concatenate([back_ref[columns_ref[j, r]] for j in range(per_row)], axis=1)
        right = jnp.concatenate([tiles_ref[r, j] for j in range(per_row)], axis=1)
        field = lax.dot_general(left, right, NT, preferred_element_type=F32)
        cols = pl.ds(pl.multiple_of(r * tile, tile), tile)
        total = members_ref[0, :, cols].astype(F32) * field[:lev_dev]
        for m in range(1, mem_dev):
            total = total + members_ref[m, :, cols].astype(F32) * field[m * lev_dev : (m + 1) * lev_dev]
        return total

    wide = out_ref.shape[2] // tile

    def forward_step(g, carry):
        for k in range(wide):
            out_ref[g, :, k * tile : (k + 1) * tile] = forward_row(g * wide + k).astype(out_ref.dtype)
        return carry

    lax.fori_loop(0, blocks // wide, forward_step, 0, unroll=32)


def full_sum(value):
    return jnp.sum(jnp.sum(value, axis=0, keepdims=True), axis=1, keepdims=True)


def image_kernel(parts_ref, own_ref, residual_ref, image_ref, sums_ref, *, scale):
    total = parts_ref[0].astype(F32)
    for i in range(1, parts_ref.shape[0]):
        total = total + parts_ref[i].astype(F32)
    own = own_ref[...]
    residual = residual_ref[...]
    image = own + total / scale
    image_ref[...] = image
    rr = full_sum(residual * residual)
    di = full_sum(own * image)
    ii = full_sum(image * image)
    ri = full_sum(residual * image)
    guess = jnp.where(ii > 0.0, ri / jnp.where(ii > 0.0, ii, 1.0), 0.0)
    left = residual - guess * image
    ll = full_sum(left * left)
    li = full_sum(left * image)
    lane = lax.broadcasted_iota(jnp.int32, (1, sums_ref.shape[1]), 1)
    row = jnp.zeros(lane.shape, F32)
    for k, value in enumerate((rr, di, ll, li, ii, guess)):
        row = jnp.where(lane == k, value, row)
    sums_ref[...] = jnp.broadcast_to(row, sums_ref.shape)


def update_kernel(parts_ref, own_ref, residual_ref, iterate_ref, image_ref, x_ref, r_ref, d_ref):
    parts = parts_ref[...]
    sums = jnp.sum(parts, axis=0, keepdims=True)
    norm_old = sums[:, 0:1]
    alpha = norm_old / sums[:, 1:2]
    ll, li, ii, guess = (parts[:, k : k + 1] for k in range(2, 6))
    shift = guess - alpha
    norm_new = jnp.sum(ll + shift * (2.0 * li + shift * ii), axis=0, keepdims=True)
    own = own_ref[...]
    residual_new = residual_ref[...] - alpha * image_ref[...]
    x_ref[...] = iterate_ref[...] + alpha * own
    r_ref[...] = residual_new
    d_ref[...] = residual_new + (norm_new / norm_old) * own


def on_device(members, direction, residual, iterate, tiles, columns, vertical):
    mem_dev, lev_dev, points = members.shape
    blocks, per_row, tile = tiles.shape[:3]
    vectors = mem_dev * lev_dev
    groups, slabs = lax.axis_size("member"), lax.axis_size("slab")
    share = points // groups
    member_count = mem_dev * groups
    levels, width = vertical.shape
    square = (lev_dev, share)
    edge = (mem_dev * HALO, points)

    far = functools.partial(pltpu.with_memory_space_constraint, memory_space=pltpu.HBM)
    near = functools.partial(pltpu.with_memory_space_constraint, memory_space=pltpu.VMEM)
    limit = pltpu.CompilerParams(vmem_limit_bytes=32 * 2**20)
    low, high, members_near = pl.pallas_call(
        edge_kernel,
        out_shape=(pltpu.VMEM(edge, BF16), pltpu.VMEM(edge, BF16), pltpu.VMEM(members.shape, BF16)),
        in_specs=[HBM, HBM],
        out_specs=(VMEM,) * 3,
        scratch_shapes=[pltpu.VMEM((2, HALO, points), F32), pltpu.SemaphoreType.DMA((3 * EDGE_CHUNKS,))],
        compiler_params=limit,
        name="edge",
    )(far(members), far(direction))
    below = lax.ppermute(high, "slab", [(i, (i + 1) % slabs) for i in range(slabs)])
    above = lax.ppermute(low, "slab", [((i + 1) % slabs, i) for i in range(slabs)])

    tiles_near, direction_near, residual_near, iterate_near, own, band = pl.pallas_call(
        functools.partial(stage_kernel, mem_dev=mem_dev),
        out_shape=(
            pltpu.VMEM(tiles.shape, BF16), pltpu.VMEM(direction.shape, F32),
            pltpu.VMEM(square, F32), pltpu.VMEM(square, F32), pltpu.VMEM(square, F32),
            pltpu.VMEM((3 * vectors, vectors + 2 * mem_dev * HALO), BF16),
        ),
        in_specs=[VMEM] + [HBM] * 4,
        out_specs=(VMEM,) * 6,
        scratch_shapes=[
            pltpu.VMEM((-(-width // 8) * 8, levels + 2 * LANES), F32),
            pltpu.SemaphoreType.DMA((4 + TILE_CHUNKS,)),
        ],
        compiler_params=limit,
        cost_estimate=pl.CostEstimate(flops=0, bytes_accessed=2 * tiles.size * 2, transcendentals=0),
        name="stage",
    )(vertical.T, far(direction), far(tiles), far(residual), far(iterate))

    partial_value = pl.pallas_call(
        product_kernel,
        out_shape=pltpu.VMEM((groups, lev_dev, share), BF16),
        in_specs=[HBM] + [VMEM] * 6,
        out_specs=VMEM,
        scratch_shapes=[
            pltpu.SMEM((per_row, blocks), jnp.int32),
            pltpu.VMEM((blocks, vectors, tile), BF16),
            pltpu.VMEM((blocks, vectors, tile), F32),
            pltpu.VMEM((blocks, vectors, tile), BF16),
            pltpu.SemaphoreType.DMA,
        ],
        compiler_params=limit,
        name="product",
    )(far(columns.T), band, members_near, direction_near, below, above, tiles_near)

    parts = lax.all_to_all(partial_value, "member", 0, 0, tiled=True)
    devices = groups * slabs
    image, sums = pl.pallas_call(
        functools.partial(image_kernel, scale=float(member_count - 1)),
        out_shape=(pltpu.VMEM(square, F32), pltpu.VMEM((devices, 128), F32)),
        in_specs=[VMEM] * 3,
        out_specs=(VMEM,) * 2,
        compiler_params=limit,
        name="image",
    )(near(parts), own, residual_near)

    spread = lax.all_to_all(sums.reshape(devices, 1, 128), ("member", "slab"), 0, 0, tiled=True)
    field = jax.ShapeDtypeStruct(square, F32)
    return pl.pallas_call(
        update_kernel,
        out_shape=(field, field, field),
        in_specs=[VMEM] * 5,
        out_specs=(VMEM,) * 3,
        compiler_params=limit,
        name="update",
    )(near(spread.reshape(devices, 128)), own, residual_near, iterate_near, image)


def solution(mesh):
    placed = (
        P("member", "slab", None),
        P("slab", None),
        P("slab", "member"),
        P("slab", "member"),
        P(),
        P(),
        P(),
    )
    return jax.shard_map(
        on_device,
        mesh=mesh,
        in_specs=placed,
        out_specs=(P("slab", "member"), P("slab", "member"), P("slab", "member")),
        check_vma=False,
    )
```

```python
import functools

import jax
import jax.numpy as jnp
from jax import lax
from jax.experimental import pallas as pl
from jax.experimental.pallas import tpu as pltpu
from jax.sharding import PartitionSpec as P

REACH = 4
HALO = 2 * REACH
EDGE_CHUNKS = 4
TILE_CHUNKS = 8
LANES = 128
NEAR = 4
F32 = jnp.float32
BF16 = jnp.bfloat16
NT = (((1,), (1,)), ((), ()))
VMEM = pl.BlockSpec(memory_space=pltpu.VMEM)
HBM = pl.BlockSpec(memory_space=pltpu.HBM)


def edge_kernel(members_hbm, direction_hbm, low_ref, high_ref, members_ref, rim_ref, sems):
    mem_dev, lev_dev, points = members_ref.shape
    step = points // EDGE_CHUNKS

    def copies(i):
        cols = pl.ds(i * step, step)
        last = pl.ds(lev_dev - HALO, HALO)
        return (
            pltpu.make_async_copy(direction_hbm.at[pl.ds(0, HALO), cols], rim_ref.at[0, :, cols], sems.at[3 * i]),
            pltpu.make_async_copy(direction_hbm.at[last, cols], rim_ref.at[1, :, cols], sems.at[3 * i + 1]),
            pltpu.make_async_copy(members_hbm.at[:, :, cols], members_ref.at[:, :, cols], sems.at[3 * i + 2]),
        )

    for i in range(EDGE_CHUNKS):
        for copy in copies(i):
            copy.start()
    for i in range(EDGE_CHUNKS):
        for copy in copies(i):
            copy.wait()
        cols = slice(i * step, (i + 1) * step)
        low, high = [], []
        for m in range(mem_dev):
            low.append(members_ref[m, : 2 * HALO, cols].astype(F32)[:HALO] * rim_ref[0, :, cols])
            high.append(members_ref[m, lev_dev - 2 * HALO :, cols].astype(F32)[HALO:] * rim_ref[1, :, cols])
        low_ref[:, cols] = jnp.concatenate(low, axis=0).astype(BF16)
        high_ref[:, cols] = jnp.concatenate(high, axis=0).astype(BF16)


def split3(value):
    high = value.astype(BF16)
    rest = value - high.astype(F32)
    middle = rest.astype(BF16)
    low = (rest - middle.astype(F32)).astype(BF16)
    return jnp.concatenate([high, middle, low], axis=0)


def level_matrix(band, level_start, levels, lev_dev, mem_dev):
    span = band.shape[0]
    lanes = 128
    row = lax.broadcasted_iota(jnp.int32, (span, lanes), 0)
    col = lax.broadcasted_iota(jnp.int32, (span, lanes), 1)
    dense = jnp.zeros((span, lanes), F32)
    for offset in range(2 * REACH + 1):
        dense = jnp.where(col == row + offset, band[:, offset : offset + 1], dense)
    level = col + (level_start - HALO - REACH)
    dense = jnp.where((level >= 0) & (level < levels), dense, 0.0)
    own, low, high = dense[HALO : HALO + lev_dev], dense[:HALO], dense[HALO + lev_dev :]
    rows = jnp.concatenate([own] * mem_dev, axis=0)
    cols = jnp.concatenate([own] * mem_dev + [low] * mem_dev + [high] * mem_dev, axis=0)
    both = lax.dot_general(rows, cols, NT, precision=lax.Precision.HIGHEST, preferred_element_type=F32)
    i = lax.broadcasted_iota(jnp.int32, both.shape, 0)
    j = lax.broadcasted_iota(jnp.int32, both.shape, 1)
    keep = jnp.zeros(both.shape, jnp.bool_)
    vectors = mem_dev * lev_dev
    for m in range(mem_dev):
        mine = (i >= m * lev_dev) & (i < (m + 1) * lev_dev)
        theirs = (j >= m * lev_dev) & (j < (m + 1) * lev_dev)
        for first in (vectors + m * HALO, vectors + (mem_dev + m) * HALO):
            theirs = theirs | ((j >= first) & (j < first + HALO))
        keep = keep | (mine & theirs)
    return jnp.where(keep, both, 0.0)


def stage_kernel(
    vertical_ref, direction_hbm, tiles_hbm, residual_hbm, iterate_hbm,
    tiles_ref, direction_ref, residual_ref, iterate_ref, own_ref, band_ref, padded_ref, sems,
    *, mem_dev,
):
    lev_dev, share = own_ref.shape
    mine = pl.ds(pl.multiple_of(lax.axis_index("member") * share, share), share)
    copies = [
        pltpu.make_async_copy(direction_hbm, direction_ref, sems.at[0]),
        pltpu.make_async_copy(direction_hbm.at[:, mine], own_ref, sems.at[1]),
        pltpu.make_async_copy(residual_hbm, residual_ref, sems.at[2]),
        pltpu.make_async_copy(iterate_hbm, iterate_ref, sems.at[3]),
    ]
    part = tiles_ref.shape[0] // TILE_CHUNKS
    for i in range(TILE_CHUNKS):
        rows = pl.ds(i * part, part)
        copies.append(pltpu.make_async_copy(tiles_hbm.at[rows], tiles_ref.at[rows], sems.at[4 + i]))
    for copy in copies:
        copy.start()
    width, levels = vertical_ref.shape
    level_start = lax.axis_index("slab") * lev_dev
    padded_ref[...] = jnp.zeros_like(padded_ref)
    padded_ref[:width, LANES : LANES + levels] = vertical_ref[...]
    total = padded_ref.shape[1]
    turned = pltpu.roll(padded_ref[...], total - (LANES - HALO + level_start), 1)[:, :LANES]
    band = jnp.concatenate([turned, jnp.zeros((LANES - turned.shape[0], LANES), F32)], axis=0).T
    band_ref[...] = split3(level_matrix(band[: lev_dev + 2 * HALO], level_start, levels, lev_dev, mem_dev))
    for copy in copies:
        copy.wait()


def forward_share(g, wide, columns_ref, tiles_ref, back_ref, members_ref):
    mem_dev, lev_dev, points = members_ref.shape
    blocks, per_row, tile, _ = tiles_ref.shape
    pieces = []
    for k in range(wide):
        r = g * wide + k
        left = jnp.concatenate([back_ref[columns_ref[j, r]] for j in range(per_row)], axis=1)
        right = jnp.concatenate([tiles_ref[r, j] for j in range(per_row)], axis=1)
        field = lax.dot_general(left, right, NT, preferred_element_type=F32)
        cols = pl.ds(pl.multiple_of(r * tile, tile), tile)
        total = members_ref[0, :, cols].astype(F32) * field[:lev_dev]
        for m in range(1, mem_dev):
            total = total + members_ref[m, :, cols].astype(F32) * field[m * lev_dev : (m + 1) * lev_dev]
        pieces.append(total)
    return jnp.concatenate(pieces, axis=1)


def product_kernel(
    columns_hbm, band_ref, members_ref, direction_ref, below_ref, above_ref, tiles_ref,
    back_ref, *rest,
):
    *send_refs, columns_ref, smooth_ref, acc_ref, sem = rest
    mem_dev, lev_dev, points = members_ref.shape
    blocks, per_row, tile, _ = tiles_ref.shape
    vectors = mem_dev * lev_dev
    fetch = pltpu.make_async_copy(columns_hbm, columns_ref, sem)
    fetch.start()
    band = band_ref[...]

    def vertical_step(g, carry):
        cols = pl.ds(pl.multiple_of(g * 2 * tile, 2 * tile), 2 * tile)
        field = direction_ref[:, cols]
        mixed = [(members_ref[m, :, cols].astype(F32) * field).astype(BF16) for m in range(mem_dev)]
        stacked = jnp.concatenate(mixed + [below_ref[:, cols], above_ref[:, cols]], axis=0)
        three = jnp.dot(band, stacked, preferred_element_type=F32)
        total = (three[2 * vectors :] + three[vectors : 2 * vectors]) + three[:vectors]
        total = total.astype(BF16)
        smooth_ref[2 * g] = total[:, :tile]
        smooth_ref[2 * g + 1] = total[:, tile:]
        for k in range(2):
            acc_ref[2 * g + k] = jnp.zeros((vectors, tile), F32)
        return carry

    lax.fori_loop(0, blocks // 2, vertical_step, 0, unroll=16)
    fetch.wait()

    def adjoint_step(r, carry):
        left = smooth_ref[r]
        where = [columns_ref[j, r] for j in range(per_row)]
        right = jnp.concatenate([tiles_ref[r, j] for j in range(per_row)], axis=1)
        spread = jnp.dot(left, right, preferred_element_type=F32)
        new = [acc_ref[where[j]] + spread[:, j * tile : (j + 1) * tile] for j in range(per_row)]
        for j in range(per_row):
            acc_ref[where[j]] = new[j]
        return carry

    lax.fori_loop(0, blocks, adjoint_step, 0, unroll=16)
    back_ref[...] = acc_ref[...].astype(BF16)
    far_count, _, share = send_refs[0].shape
    here = lax.axis_index("member") % NEAR
    for d in range(1, NEAR):
        target = (here + d) % NEAR
        out_ref = send_refs[d - 1]

        def forward_step(z, carry, target=target, out_ref=out_ref):
            value = forward_share(z * NEAR + target, share // tile, columns_ref, tiles_ref, back_ref, members_ref)
            out_ref[z] = value.astype(out_ref.dtype)
            return carry

        lax.fori_loop(0, far_count, forward_step, 0, unroll=8)


def own_kernel(columns_hbm, members_ref, tiles_ref, back_ref, out_ref, columns_ref, sem):
    fetch = pltpu.make_async_copy(columns_hbm, columns_ref, sem)
    fetch.start()
    fetch.wait()
    far_count, _, share = out_ref.shape
    tile = tiles_ref.shape[3]
    here = lax.axis_index("member") % NEAR

    def forward_step(z, carry):
        out_ref[z] = forward_share(z * NEAR + here, share // tile, columns_ref, tiles_ref, back_ref, members_ref)
        return carry

    lax.fori_loop(0, far_count, forward_step, 0, unroll=8)


def fold_kernel(own_ref, *refs):
    *arrived, out_ref = refs
    total = own_ref[...]
    for ref in arrived:
        total = total + ref[...].astype(F32)
    out_ref[...] = total.astype(out_ref.dtype)


def full_sum(value):
    return jnp.sum(jnp.sum(value, axis=0, keepdims=True), axis=1, keepdims=True)


def image_kernel(parts_ref, own_ref, residual_ref, image_ref, sums_ref, *, scale):
    total = parts_ref[0].astype(F32)
    for i in range(1, parts_ref.shape[0]):
        total = total + parts_ref[i].astype(F32)
    own = own_ref[...]
    residual = residual_ref[...]
    image = own + total / scale
    image_ref[...] = image
    rr = full_sum(residual * residual)
    di = full_sum(own * image)
    ii = full_sum(image * image)
    ri = full_sum(residual * image)
    guess = jnp.where(ii > 0.0, ri / jnp.where(ii > 0.0, ii, 1.0), 0.0)
    left = residual - guess * image
    ll = full_sum(left * left)
    li = full_sum(left * image)
    lane = lax.broadcasted_iota(jnp.int32, (1, sums_ref.shape[1]), 1)
    row = jnp.zeros(lane.shape, F32)
    for k, value in enumerate((rr, di, ll, li, ii, guess)):
        row = jnp.where(lane == k, value, row)
    sums_ref[...] = jnp.broadcast_to(row, sums_ref.shape)


def update_kernel(parts_ref, own_ref, residual_ref, iterate_ref, image_ref, x_ref, r_ref, d_ref):
    parts = parts_ref[...]
    sums = jnp.sum(parts, axis=0, keepdims=True)
    norm_old = sums[:, 0:1]
    alpha = norm_old / sums[:, 1:2]
    ll, li, ii, guess = (parts[:, k : k + 1] for k in range(2, 6))
    shift = guess - alpha
    norm_new = jnp.sum(ll + shift * (2.0 * li + shift * ii), axis=0, keepdims=True)
    own = own_ref[...]
    residual_new = residual_ref[...] - alpha * image_ref[...]
    x_ref[...] = iterate_ref[...] + alpha * own
    r_ref[...] = residual_new
    d_ref[...] = residual_new + (norm_new / norm_old) * own


def on_device(members, direction, residual, iterate, tiles, columns, vertical):
    mem_dev, lev_dev, points = members.shape
    blocks, per_row, tile = tiles.shape[:3]
    vectors = mem_dev * lev_dev
    groups, slabs = lax.axis_size("member"), lax.axis_size("slab")
    share = points // groups
    member_count = mem_dev * groups
    levels, width = vertical.shape
    square = (lev_dev, share)
    edge = (mem_dev * HALO, points)

    far = functools.partial(pltpu.with_memory_space_constraint, memory_space=pltpu.HBM)
    near = functools.partial(pltpu.with_memory_space_constraint, memory_space=pltpu.VMEM)
    limit = pltpu.CompilerParams(vmem_limit_bytes=32 * 2**20)
    low, high, members_near = pl.pallas_call(
        edge_kernel,
        out_shape=(pltpu.VMEM(edge, BF16), pltpu.VMEM(edge, BF16), pltpu.VMEM(members.shape, BF16)),
        in_specs=[HBM, HBM],
        out_specs=(VMEM,) * 3,
        scratch_shapes=[pltpu.VMEM((2, HALO, points), F32), pltpu.SemaphoreType.DMA((3 * EDGE_CHUNKS,))],
        compiler_params=limit,
        name="edge",
    )(far(members), far(direction))
    below = lax.ppermute(high, "slab", [(i, (i + 1) % slabs) for i in range(slabs)])
    above = lax.ppermute(low, "slab", [((i + 1) % slabs, i) for i in range(slabs)])

    tiles_near, direction_near, residual_near, iterate_near, own, band = pl.pallas_call(
        functools.partial(stage_kernel, mem_dev=mem_dev),
        out_shape=(
            pltpu.VMEM(tiles.shape, BF16), pltpu.VMEM(direction.shape, F32),
            pltpu.VMEM(square, F32), pltpu.VMEM(square, F32), pltpu.VMEM(square, F32),
            pltpu.VMEM((3 * vectors, vectors + 2 * mem_dev * HALO), BF16),
        ),
        in_specs=[VMEM] + [HBM] * 4,
        out_specs=(VMEM,) * 6,
        scratch_shapes=[
            pltpu.VMEM((-(-width // 8) * 8, levels + 2 * LANES), F32),
            pltpu.SemaphoreType.DMA((4 + TILE_CHUNKS,)),
        ],
        compiler_params=limit,
        cost_estimate=pl.CostEstimate(flops=0, bytes_accessed=2 * tiles.size * 2, transcendentals=0),
        name="stage",
    )(vertical.T, far(direction), far(tiles), far(residual), far(iterate))

    far_count = groups // NEAR
    piece = (far_count, lev_dev, share)
    columns_far = far(columns.T)
    columns_scratch = [pltpu.SMEM((per_row, blocks), jnp.int32)]
    back, *sent = pl.pallas_call(
        product_kernel,
        out_shape=(pltpu.VMEM((blocks, vectors, tile), BF16),) + (pltpu.VMEM(piece, BF16),) * (NEAR - 1),
        in_specs=[HBM] + [VMEM] * 6,
        out_specs=(VMEM,) * NEAR,
        scratch_shapes=columns_scratch + [
            pltpu.VMEM((blocks, vectors, tile), BF16),
            pltpu.VMEM((blocks, vectors, tile), F32),
            pltpu.SemaphoreType.DMA,
        ],
        compiler_params=limit,
        name="product",
    )(columns_far, band, members_near, direction_near, below, above, tiles_near)
    arrived = [
        lax.ppermute(
            sent[d - 1], "member", [(i, i // NEAR * NEAR + (i + d) % NEAR) for i in range(groups)]
        )
        for d in range(1, NEAR)
    ]
    own_part = pl.pallas_call(
        own_kernel,
        out_shape=pltpu.VMEM(piece, F32),
        in_specs=[HBM] + [VMEM] * 3,
        out_specs=VMEM,
        scratch_shapes=columns_scratch + [pltpu.SemaphoreType.DMA],
        compiler_params=limit,
        cost_estimate=pl.CostEstimate(flops=vectors * points * per_row * tile // 2, bytes_accessed=tiles.size // 2, transcendentals=0),
        name="own",
    )(columns_far, members_near, tiles_near, back)
    folded = pl.pallas_call(
        fold_kernel,
        out_shape=pltpu.VMEM(piece, BF16),
        in_specs=[VMEM] * NEAR,
        out_specs=VMEM,
        compiler_params=limit,
        name="fold",
    )(near(own_part), *(near(x) for x in arrived))
    columns_of = [[y + NEAR * z for z in range(far_count)] for y in range(NEAR)]
    parts = lax.all_to_all(folded, "member", 0, 0, axis_index_groups=columns_of, tiled=True)
    devices = groups * slabs
    image, sums = pl.pallas_call(
        functools.partial(image_kernel, scale=float(member_count - 1)),
        out_shape=(pltpu.VMEM(square, F32), pltpu.VMEM((devices, 128), F32)),
        in_specs=[VMEM] * 3,
        out_specs=(VMEM,) * 2,
        compiler_params=limit,
        name="image",
    )(near(parts), own, residual_near)

    spread = lax.all_to_all(sums.reshape(devices, 1, 128), ("member", "slab"), 0, 0, tiled=True)
    field = jax.ShapeDtypeStruct(square, F32)
    return pl.pallas_call(
        update_kernel,
        out_shape=(field, field, field),
        in_specs=[VMEM] * 5,
        out_specs=(VMEM,) * 3,
        compiler_params=limit,
        name="update",
    )(near(spread.reshape(devices, 128)), own, residual_near, iterate_near, image)


def solution(mesh):
    placed = (
        P("member", "slab", None),
        P("slab", None),
        P("slab", "member"),
        P("slab", "member"),
        P(),
        P(),
        P(),
    )
    return jax.shard_map(
        on_device,
        mesh=mesh,
        in_specs=placed,
        out_specs=(P("slab", "member"), P("slab", "member"), P("slab", "member")),
        check_vma=False,
    )
```

```python
import functools

import jax
import jax.numpy as jnp
from jax import lax
from jax.experimental import pallas as pl
from jax.experimental.pallas import tpu as pltpu
from jax.sharding import PartitionSpec as P

REACH = 4
HALO = 2 * REACH
EDGE_CHUNKS = 2
EARLY_SHARE = 2
LATE_CHUNKS = 6
LANES = 128
NEAR = 4
F32 = jnp.float32
BF16 = jnp.bfloat16
NT = (((1,), (1,)), ((), ()))
VMEM = pl.BlockSpec(memory_space=pltpu.VMEM)
HBM = pl.BlockSpec(memory_space=pltpu.HBM)


def link_kernel(members_hbm, direction_hbm, link_ref, part_ref, rim_ref, sems):
    mem_dev, near_rows, points = part_ref.shape
    lev_dev = direction_hbm.shape[0]
    step = points // EDGE_CHUNKS
    odd = lax.axis_index("slab") % 2
    first = pl.multiple_of(odd * (lev_dev - near_rows), near_rows)
    first_rim = pl.multiple_of(odd * (lev_dev - HALO), HALO)

    def copies(i):
        cols = pl.ds(i * step, step)
        return (
            pltpu.make_async_copy(direction_hbm.at[pl.ds(first_rim, HALO), cols], rim_ref.at[:, cols], sems.at[2 * i]),
            pltpu.make_async_copy(
                members_hbm.at[:, pl.ds(first, near_rows), cols], part_ref.at[:, :, cols], sems.at[2 * i + 1]
            ),
        )

    for i in range(EDGE_CHUNKS):
        for copy in copies(i):
            copy.start()
    for i in range(EDGE_CHUNKS):
        for copy in copies(i):
            copy.wait()
        cols = slice(i * step, (i + 1) * step)
        rows = []
        for m in range(mem_dev):
            near = part_ref[m, :, cols].astype(F32)
            rows.append(jnp.where(odd == 1, near[near_rows - HALO :], near[:HALO]) * rim_ref[:, cols])
        link_ref[:, cols] = jnp.concatenate(rows, axis=0).astype(BF16)


def split3(value):
    high = value.astype(BF16)
    rest = value - high.astype(F32)
    middle = rest.astype(BF16)
    low = (rest - middle.astype(F32)).astype(BF16)
    return jnp.concatenate([high, middle, low], axis=0)


def level_matrix(band, even, level_start, levels, lev_dev, mem_dev):
    span = band.shape[0]
    lanes = 128
    row = lax.broadcasted_iota(jnp.int32, (span, lanes), 0)
    col = lax.broadcasted_iota(jnp.int32, (span, lanes), 1)
    dense = jnp.zeros((span, lanes), F32)
    for offset in range(2 * REACH + 1):
        dense = jnp.where(col == row + offset, band[:, offset : offset + 1], dense)
    level = col + (level_start - HALO - REACH)
    dense = jnp.where((level >= 0) & (level < levels), dense, 0.0)
    own, low, high = dense[HALO : HALO + lev_dev], dense[:HALO], dense[HALO + lev_dev :]
    chip, link = jnp.where(even, high, low), jnp.where(even, low, high)
    rows = jnp.concatenate([own] * mem_dev, axis=0)
    cols = jnp.concatenate([own] * mem_dev + [chip] * mem_dev + [link] * mem_dev, axis=0)
    both = lax.dot_general(rows, cols, NT, precision=lax.Precision.HIGHEST, preferred_element_type=F32)
    i = lax.broadcasted_iota(jnp.int32, both.shape, 0)
    j = lax.broadcasted_iota(jnp.int32, both.shape, 1)
    keep = jnp.zeros(both.shape, jnp.bool_)
    vectors = mem_dev * lev_dev
    for m in range(mem_dev):
        mine = (i >= m * lev_dev) & (i < (m + 1) * lev_dev)
        theirs = (j >= m * lev_dev) & (j < (m + 1) * lev_dev)
        for first in (vectors + m * HALO, vectors + (mem_dev + m) * HALO):
            theirs = theirs | ((j >= first) & (j < first + HALO))
        keep = keep | (mine & theirs)
    both = jnp.where(keep, both, 0.0)
    inner, rim = [], []
    for m in range(mem_dev):
        first, last = m * lev_dev, (m + 1) * lev_dev
        inner.append(both[first + HALO : last - HALO])
        rim += [both[first : first + HALO], both[last - HALO : last]]
    return jnp.concatenate(inner, axis=0)[:, :vectors], jnp.concatenate(rim, axis=0)


def vertical_pass(band, fields, blocks, tile, smooth_ref, acc_ref=None):
    rows = band.shape[0] // 3

    def step(g, carry):
        cols = pl.ds(pl.multiple_of(g * 2 * tile, 2 * tile), 2 * tile)
        three = jnp.dot(band, fields(cols), preferred_element_type=F32)
        total = (three[2 * rows :] + three[rows : 2 * rows]) + three[:rows]
        total = total.astype(BF16)
        for k in range(2):
            smooth_ref[2 * g + k] = total[:, k * tile : (k + 1) * tile]
            if acc_ref is not None:
                acc_ref[2 * g + k] = jnp.zeros((rows, tile), F32)
        return carry

    lax.fori_loop(0, blocks // 2, step, 0, unroll=16)


def adjoint_pass(first, last, base, columns_ref, tiles_ref, smooth_ref, acc_ref, unroll):
    per_row, tile = tiles_ref.shape[1], tiles_ref.shape[3]

    def step(r, carry):
        where = [columns_ref[j, r] for j in range(per_row)]
        right = jnp.concatenate([tiles_ref[r - base, j] for j in range(per_row)], axis=1)
        spread = jnp.dot(smooth_ref[r], right, preferred_element_type=F32)
        new = [acc_ref[where[j]] + spread[:, j * tile : (j + 1) * tile] for j in range(per_row)]
        for j in range(per_row):
            acc_ref[where[j]] = new[j]
        return carry

    lax.fori_loop(first, last, step, 0, unroll=unroll)


def smooth_kernel(
    vertical_hbm, direction_hbm, members_hbm, residual_hbm, iterate_hbm, columns_hbm, tiles_hbm,
    members_ref, mixed_ref, residual_ref, iterate_ref, own_ref, band_ref, table_ref, smooth_ref, chip_ref, tiles_ref,
    vertical_ref, padded_ref, direction_ref, sems,
):
    mem_dev, lev_dev, points = members_ref.shape
    blocks, _, tile = smooth_ref.shape
    share = own_ref.shape[1]
    mine = pl.ds(pl.multiple_of(lax.axis_index("member") * share, share), share)
    pairs = [
        (vertical_hbm, vertical_ref),
        (direction_hbm, direction_ref),
        (members_hbm, members_ref),
        (columns_hbm, table_ref),
        (tiles_hbm.at[pl.ds(0, tiles_ref.shape[0])], tiles_ref),
        (direction_hbm.at[:, mine], own_ref),
        (residual_hbm, residual_ref),
        (iterate_hbm, iterate_ref),
    ]
    copies = [pltpu.make_async_copy(source, target, sems.at[i]) for i, (source, target) in enumerate(pairs)]
    for copy in copies:
        copy.start()
    width, levels = vertical_ref.shape
    slab = lax.axis_index("slab")
    level_start = slab * lev_dev
    even = slab % 2 == 0
    padded_ref[...] = jnp.zeros_like(padded_ref)
    copies[0].wait()
    for i in range(width):
        padded_ref[i : i + 1, LANES : LANES + levels] = vertical_ref[i : i + 1, :]
    total = padded_ref.shape[1]
    turned = pltpu.roll(padded_ref[...], total - (LANES - HALO + level_start), 1)[:, :LANES]
    band = jnp.concatenate([turned, jnp.zeros((LANES - turned.shape[0], LANES), F32)], axis=0).T
    inner, rim = level_matrix(band[: lev_dev + 2 * HALO], even, level_start, levels, lev_dev, mem_dev)
    band_ref[...] = split3(rim)
    copies[1].wait()
    copies[2].wait()

    def fields(cols):
        field = direction_ref[:, cols]
        wide = [members_ref[m, :, cols].astype(F32) * field for m in range(mem_dev)]
        low = jnp.concatenate([x[:HALO] for x in wide], axis=0)
        high = jnp.concatenate([x[lev_dev - HALO :] for x in wide], axis=0)
        chip_ref[:, cols] = jnp.where(even, high, low).astype(BF16)
        mixed = jnp.concatenate(wide, axis=0).astype(BF16)
        mixed_ref[:, cols] = mixed
        return mixed

    vertical_pass(split3(inner), fields, blocks, tile, smooth_ref)
    for copy in copies[3:]:
        copy.wait()


def interior_kernel(table_ref, smooth_ref, early_ref, tiles_hbm, late_ref, inner_ref, columns_ref, acc_ref, sems):
    early, late = early_ref.shape[0], late_ref.shape[0]
    part = late // LATE_CHUNKS
    copies = [
        pltpu.make_async_copy(
            tiles_hbm.at[pl.ds(early + i * part, part)], late_ref.at[pl.ds(i * part, part)], sems.at[i]
        )
        for i in range(LATE_CHUNKS)
    ]
    fetch = pltpu.make_async_copy(table_ref, columns_ref, sems.at[LATE_CHUNKS])
    fetch.start()
    for copy in copies:
        copy.start()
    acc_ref[...] = jnp.zeros_like(acc_ref)
    fetch.wait()
    adjoint_pass(0, early, 0, columns_ref, early_ref, smooth_ref, acc_ref, 8)
    for i, copy in enumerate(copies):
        copy.wait()
        adjoint_pass(early + i * part, early + (i + 1) * part, early, columns_ref, late_ref, smooth_ref, acc_ref, 8)
    inner_ref[...] = acc_ref[...].astype(BF16)


def forward_share(g, wide, base, columns_ref, tiles_ref, inner_ref, rim_ref, members_ref):
    mem_dev, lev_dev, points = members_ref.shape
    blocks, per_row, tile, _ = tiles_ref.shape
    middle = lev_dev - 2 * HALO
    pieces = []
    for k in range(wide):
        r = g * wide + k
        left = []
        for j in range(per_row):
            c = columns_ref[j, r]
            left.append(jnp.concatenate([inner_ref[c], rim_ref[c]], axis=0))
        right = jnp.concatenate([tiles_ref[r - base, j] for j in range(per_row)], axis=1)
        field = lax.dot_general(jnp.concatenate(left, axis=1), right, NT, preferred_element_type=F32)
        cols = pl.ds(pl.multiple_of(r * tile, tile), tile)
        total = jnp.zeros((lev_dev, tile), F32)
        for m in range(mem_dev):
            inside = field[m * middle : (m + 1) * middle]
            low = mem_dev * middle + 2 * m * HALO
            levels = jnp.concatenate([field[low : low + HALO], inside, field[low + HALO : low + 2 * HALO]], axis=0)
            total = total + members_ref[m, :, cols].astype(F32) * levels
        pieces.append(total)
    return jnp.concatenate(pieces, axis=1)


def forward_shares(shifts, columns_ref, early_ref, late_ref, inner_ref, rim_ref, members_ref, out_refs):
    far_count, _, share = out_refs[0].shape
    early = early_ref.shape[0]
    wide = share // early_ref.shape[3]
    here = lax.axis_index("member") % NEAR
    for shift, out_ref in zip(shifts, out_refs):
        target = (here + shift) % NEAR
        for z in range(far_count):
            in_early = (z + 1) * NEAR * wide <= early
            base, tiles_ref = (0, early_ref) if in_early else (early, late_ref)
            value = forward_share(z * NEAR + target, wide, base, columns_ref, tiles_ref, inner_ref, rim_ref, members_ref)
            out_ref[z] = value.astype(out_ref.dtype)


def product_kernel(
    table_ref, band_ref, members_ref, mixed_ref, inner_ref, chip_ref, link_ref, early_ref, late_ref,
    rim_ref, *rest, shifts,
):
    *out_refs, columns_ref, smooth_ref, acc_ref, sem = rest
    early, _, tile, _ = early_ref.shape
    blocks = early + late_ref.shape[0]
    fetch = pltpu.make_async_copy(table_ref, columns_ref, sem)
    fetch.start()

    def fields(cols):
        return jnp.concatenate([mixed_ref[:, cols], chip_ref[:, cols], link_ref[:, cols]], axis=0)

    vertical_pass(band_ref[...], fields, blocks, tile, smooth_ref, acc_ref)
    fetch.wait()
    adjoint_pass(0, early, 0, columns_ref, early_ref, smooth_ref, acc_ref, 16)
    adjoint_pass(early, blocks, early, columns_ref, late_ref, smooth_ref, acc_ref, 16)
    rim_ref[...] = acc_ref[...].astype(BF16)
    forward_shares(shifts, columns_ref, early_ref, late_ref, inner_ref, rim_ref, members_ref, out_refs)


def share_kernel(table_ref, members_ref, early_ref, late_ref, inner_ref, rim_ref, *rest, shifts):
    *out_refs, columns_ref, sem = rest
    fetch = pltpu.make_async_copy(table_ref, columns_ref, sem)
    fetch.start()
    fetch.wait()
    forward_shares(shifts, columns_ref, early_ref, late_ref, inner_ref, rim_ref, members_ref, out_refs)


def fold_kernel(own_ref, *refs):
    *arrived, out_ref = refs
    total = own_ref[...]
    for ref in arrived:
        total = total + ref[...].astype(F32)
    out_ref[...] = total.astype(out_ref.dtype)


def full_sum(value):
    return jnp.sum(jnp.sum(value, axis=0, keepdims=True), axis=1, keepdims=True)


def image_kernel(parts_ref, own_ref, residual_ref, image_ref, sums_ref, *, scale):
    total = parts_ref[0].astype(F32)
    for i in range(1, parts_ref.shape[0]):
        total = total + parts_ref[i].astype(F32)
    own = own_ref[...]
    residual = residual_ref[...]
    image = own + total / scale
    image_ref[...] = image
    rr = full_sum(residual * residual)
    di = full_sum(own * image)
    ii = full_sum(image * image)
    ri = full_sum(residual * image)
    guess = jnp.where(ii > 0.0, ri / jnp.where(ii > 0.0, ii, 1.0), 0.0)
    left = residual - guess * image
    ll = full_sum(left * left)
    li = full_sum(left * image)
    lane = lax.broadcasted_iota(jnp.int32, (1, sums_ref.shape[1]), 1)
    row = jnp.zeros(lane.shape, F32)
    for k, value in enumerate((rr, di, ll, li, ii, guess)):
        row = jnp.where(lane == k, value, row)
    sums_ref[...] = jnp.broadcast_to(row, sums_ref.shape)


def update_kernel(parts_ref, own_ref, residual_ref, iterate_ref, image_ref, x_ref, r_ref, d_ref):
    parts = parts_ref[...]
    sums = jnp.sum(parts, axis=0, keepdims=True)
    norm_old = sums[:, 0:1]
    alpha = norm_old / sums[:, 1:2]
    ll, li, ii, guess = (parts[:, k : k + 1] for k in range(2, 6))
    shift = guess - alpha
    norm_new = jnp.sum(ll + shift * (2.0 * li + shift * ii), axis=0, keepdims=True)
    own = own_ref[...]
    residual_new = residual_ref[...] - alpha * image_ref[...]
    x_ref[...] = iterate_ref[...] + alpha * own
    r_ref[...] = residual_new
    d_ref[...] = residual_new + (norm_new / norm_old) * own


def on_device(members, direction, residual, iterate, tiles, columns, vertical):
    mem_dev, lev_dev, points = members.shape
    blocks, per_row, tile = tiles.shape[:3]
    vectors = mem_dev * lev_dev
    groups, slabs = lax.axis_size("member"), lax.axis_size("slab")
    share = points // groups
    member_count = mem_dev * groups
    levels, width = vertical.shape
    square = (lev_dev, share)
    edge = (mem_dev * HALO, points)

    far = functools.partial(pltpu.with_memory_space_constraint, memory_space=pltpu.HBM)
    near = functools.partial(pltpu.with_memory_space_constraint, memory_space=pltpu.VMEM)
    limit = pltpu.CompilerParams(vmem_limit_bytes=32 * 2**20)
    to_link, = pl.pallas_call(
        link_kernel,
        out_shape=(pltpu.VMEM(edge, BF16),),
        in_specs=[HBM, HBM],
        out_specs=(VMEM,),
        scratch_shapes=[
            pltpu.VMEM((mem_dev, 2 * HALO, points), BF16),
            pltpu.VMEM((HALO, points), F32),
            pltpu.SemaphoreType.DMA((2 * EDGE_CHUNKS,)),
        ],
        compiler_params=limit,
        name="link_edge",
    )(far(members), far(direction))
    pairs = [(i, (i + 1) % slabs) for i in range(1, slabs, 2)]
    link = lax.ppermute(to_link, "slab", pairs + [(target, source) for source, target in pairs])

    rim_rows = 2 * mem_dev * HALO
    inner_rows = vectors - rim_rows
    columns_scratch = pltpu.SMEM((per_row, blocks), jnp.int32)
    early = EARLY_SHARE * blocks // 8
    late = blocks - early
    (
        members_near, mixed, residual_near, iterate_near, own, band, columns_near, smooth, to_chip, tiles_early,
    ) = pl.pallas_call(
        smooth_kernel,
        out_shape=(
            pltpu.VMEM(members.shape, BF16), pltpu.VMEM((vectors, points), BF16),
            pltpu.VMEM(square, F32), pltpu.VMEM(square, F32), pltpu.VMEM(square, F32),
            pltpu.VMEM((3 * rim_rows, vectors + rim_rows), BF16),
            pltpu.VMEM((per_row, blocks), jnp.int32),
            pltpu.VMEM((blocks, inner_rows, tile), BF16),
            pltpu.VMEM(edge, BF16),
            pltpu.VMEM((early,) + tiles.shape[1:], BF16),
        ),
        in_specs=[HBM] * 7,
        out_specs=(VMEM,) * 10,
        scratch_shapes=[
            pltpu.VMEM((width, levels), F32),
            pltpu.VMEM((-(-width // 8) * 8, levels + 2 * LANES), F32),
            pltpu.VMEM(direction.shape, F32),
            pltpu.SemaphoreType.DMA((8,)),
        ],
        compiler_params=limit,
        cost_estimate=pl.CostEstimate(flops=0, bytes_accessed=tiles.size // 2, transcendentals=0),
        name="smooth",
    )(far(vertical.T), far(direction), far(members), far(residual), far(iterate), far(columns.T), far(tiles))
    chip = lax.ppermute(to_chip, "slab", [(i, i ^ 1) for i in range(slabs)])
    tiles_late, inner = pl.pallas_call(
        interior_kernel,
        out_shape=(pltpu.VMEM((late,) + tiles.shape[1:], BF16), pltpu.VMEM((blocks, inner_rows, tile), BF16)),
        in_specs=[VMEM] * 3 + [HBM],
        out_specs=(VMEM,) * 2,
        scratch_shapes=[
            columns_scratch,
            pltpu.VMEM((blocks, inner_rows, tile), F32),
            pltpu.SemaphoreType.DMA((LATE_CHUNKS + 1,)),
        ],
        compiler_params=limit,
        cost_estimate=pl.CostEstimate(
            flops=2 * inner_rows * points * per_row * tile, bytes_accessed=2 * tiles.size * 2, transcendentals=0
        ),
        name="interior",
    )(columns_near, smooth, tiles_early, far(tiles))

    far_count = groups // NEAR
    piece = (far_count, lev_dev, share)
    flops = 2 * vectors * points * per_row * tile

    def shares(shifts, dtype, name):
        return pl.pallas_call(
            functools.partial(share_kernel, shifts=shifts),
            out_shape=(pltpu.VMEM(piece, dtype),) * len(shifts),
            in_specs=[VMEM] * 6,
            out_specs=(VMEM,) * len(shifts),
            scratch_shapes=[columns_scratch, pltpu.SemaphoreType.DMA],
            compiler_params=limit,
            cost_estimate=pl.CostEstimate(
                flops=flops * len(shifts) // NEAR, bytes_accessed=tiles.size * 2 * len(shifts) // NEAR, transcendentals=0
            ),
            name=name,
        )(columns_near, members_near, tiles_early, tiles_late, inner, rim)

    def send(value, shift):
        return lax.ppermute(value, "member", [(i, i // NEAR * NEAR + (i + shift) % NEAR) for i in range(groups)])

    early, late = (1, 3, 2), ()
    rim, *sent = pl.pallas_call(
        functools.partial(product_kernel, shifts=early),
        out_shape=(pltpu.VMEM((blocks, rim_rows, tile), BF16),) + (pltpu.VMEM(piece, BF16),) * len(early),
        in_specs=[VMEM] * 9,
        out_specs=(VMEM,) * (1 + len(early)),
        scratch_shapes=[
            columns_scratch,
            pltpu.VMEM((blocks, rim_rows, tile), BF16),
            pltpu.VMEM((blocks, rim_rows, tile), F32),
            pltpu.SemaphoreType.DMA,
        ],
        compiler_params=limit,
        name="product",
    )(columns_near, band, members_near, mixed, inner, chip, link, tiles_early, tiles_late)
    arrived = [send(value, shift) for value, shift in zip(sent, early)]
    own_part, = shares((0,), F32, "own")
    folded = pl.pallas_call(
        fold_kernel,
        out_shape=pltpu.VMEM(piece, BF16),
        in_specs=[VMEM] * NEAR,
        out_specs=VMEM,
        compiler_params=limit,
        name="fold",
    )(near(own_part), *(near(x) for x in arrived))
    columns_of = [[y + NEAR * z for z in range(far_count)] for y in range(NEAR)]
    parts = lax.all_to_all(folded, "member", 0, 0, axis_index_groups=columns_of, tiled=True)
    devices = groups * slabs
    image, sums = pl.pallas_call(
        functools.partial(image_kernel, scale=float(member_count - 1)),
        out_shape=(pltpu.VMEM(square, F32), pltpu.VMEM((devices, 128), F32)),
        in_specs=[VMEM] * 3,
        out_specs=(VMEM,) * 2,
        compiler_params=limit,
        name="image",
    )(near(parts), own, residual_near)

    spread = lax.all_to_all(sums.reshape(devices, 1, 128), ("member", "slab"), 0, 0, tiled=True)
    field = jax.ShapeDtypeStruct(square, F32)
    return pl.pallas_call(
        update_kernel,
        out_shape=(field, field, field),
        in_specs=[VMEM] * 5,
        out_specs=(VMEM,) * 3,
        compiler_params=limit,
        name="update",
    )(near(spread.reshape(devices, 128)), own, residual_near, iterate_near, image)


def solution(mesh):
    placed = (
        P("member", "slab", None),
        P("slab", None),
        P("slab", "member"),
        P("slab", "member"),
        P(),
        P(),
        P(),
    )
    return jax.shard_map(
        on_device,
        mesh=mesh,
        in_specs=placed,
        out_specs=(P("slab", "member"), P("slab", "member"), P("slab", "member")),
        check_vma=False,
    )
```

```python
import functools

import jax
import jax.numpy as jnp
from jax import lax
from jax.experimental import pallas as pl
from jax.experimental.pallas import tpu as pltpu
from jax.sharding import PartitionSpec as P

REACH = 4
HALO = 2 * REACH
EDGE_CHUNKS = 2
EARLY_SHARE = 2
LATE_CHUNKS = 6
LANES = 128
NEAR = 4
F32 = jnp.float32
BF16 = jnp.bfloat16
NT = (((1,), (1,)), ((), ()))
VMEM = pl.BlockSpec(memory_space=pltpu.VMEM)
HBM = pl.BlockSpec(memory_space=pltpu.HBM)


def link_kernel(members_hbm, direction_hbm, link_ref, part_ref, rim_ref, sems):
    mem_dev, near_rows, points = part_ref.shape
    lev_dev = direction_hbm.shape[0]
    step = points // EDGE_CHUNKS
    odd = lax.axis_index("slab") % 2
    first = pl.multiple_of(odd * (lev_dev - near_rows), near_rows)
    first_rim = pl.multiple_of(odd * (lev_dev - HALO), HALO)

    def copies(i):
        cols = pl.ds(i * step, step)
        return (
            pltpu.make_async_copy(direction_hbm.at[pl.ds(first_rim, HALO), cols], rim_ref.at[:, cols], sems.at[2 * i]),
            pltpu.make_async_copy(
                members_hbm.at[:, pl.ds(first, near_rows), cols], part_ref.at[:, :, cols], sems.at[2 * i + 1]
            ),
        )

    for i in range(EDGE_CHUNKS):
        for copy in copies(i):
            copy.start()
    for i in range(EDGE_CHUNKS):
        for copy in copies(i):
            copy.wait()
        cols = slice(i * step, (i + 1) * step)
        rows = []
        for m in range(mem_dev):
            near = part_ref[m, :, cols].astype(F32)
            rows.append(jnp.where(odd == 1, near[near_rows - HALO :], near[:HALO]) * rim_ref[:, cols])
        link_ref[:, cols] = jnp.concatenate(rows, axis=0).astype(BF16)


def split3(value):
    high = value.astype(BF16)
    rest = value - high.astype(F32)
    middle = rest.astype(BF16)
    low = (rest - middle.astype(F32)).astype(BF16)
    return jnp.concatenate([high, middle, low], axis=0)


def level_matrix(band, even, level_start, levels, lev_dev, mem_dev):
    span = band.shape[0]
    lanes = 128
    row = lax.broadcasted_iota(jnp.int32, (span, lanes), 0)
    col = lax.broadcasted_iota(jnp.int32, (span, lanes), 1)
    dense = jnp.zeros((span, lanes), F32)
    for offset in range(2 * REACH + 1):
        dense = jnp.where(col == row + offset, band[:, offset : offset + 1], dense)
    level = col + (level_start - HALO - REACH)
    dense = jnp.where((level >= 0) & (level < levels), dense, 0.0)
    own, low, high = dense[HALO : HALO + lev_dev], dense[:HALO], dense[HALO + lev_dev :]
    chip, link = jnp.where(even, high, low), jnp.where(even, low, high)
    rows = jnp.concatenate([own] * mem_dev, axis=0)
    cols = jnp.concatenate([own] * mem_dev + [chip] * mem_dev + [link] * mem_dev, axis=0)
    both = lax.dot_general(rows, cols, NT, precision=lax.Precision.HIGHEST, preferred_element_type=F32)
    i = lax.broadcasted_iota(jnp.int32, both.shape, 0)
    j = lax.broadcasted_iota(jnp.int32, both.shape, 1)
    keep = jnp.zeros(both.shape, jnp.bool_)
    vectors = mem_dev * lev_dev
    for m in range(mem_dev):
        mine = (i >= m * lev_dev) & (i < (m + 1) * lev_dev)
        theirs = (j >= m * lev_dev) & (j < (m + 1) * lev_dev)
        for first in (vectors + m * HALO, vectors + (mem_dev + m) * HALO):
            theirs = theirs | ((j >= first) & (j < first + HALO))
        keep = keep | (mine & theirs)
    both = jnp.where(keep, both, 0.0)
    inner, rim = [], []
    for m in range(mem_dev):
        first, last = m * lev_dev, (m + 1) * lev_dev
        inner.append(both[first + HALO : last - HALO])
        rim += [both[first : first + HALO], both[last - HALO : last]]
    return jnp.concatenate(inner, axis=0)[:, :vectors], jnp.concatenate(rim, axis=0)


def vertical_pass(band, fields, blocks, tile, smooth_ref, acc_ref=None):
    rows = band.shape[0] // 3

    def step(g, carry):
        cols = pl.ds(pl.multiple_of(g * 2 * tile, 2 * tile), 2 * tile)
        three = jnp.dot(band, fields(cols), preferred_element_type=F32)
        total = (three[2 * rows :] + three[rows : 2 * rows]) + three[:rows]
        total = total.astype(BF16)
        for k in range(2):
            smooth_ref[2 * g + k] = total[:, k * tile : (k + 1) * tile]
            if acc_ref is not None:
                acc_ref[2 * g + k] = jnp.zeros((rows, tile), F32)
        return carry

    lax.fori_loop(0, blocks // 2, step, 0, unroll=16)


def adjoint_pass(first, last, base, columns_ref, tiles_ref, smooth_ref, acc_ref, unroll):
    per_row, tile = tiles_ref.shape[1], tiles_ref.shape[3]

    def step(r, carry):
        where = [columns_ref[j, r] for j in range(per_row)]
        right = jnp.concatenate([tiles_ref[r - base, j] for j in range(per_row)], axis=1)
        spread = jnp.dot(smooth_ref[r], right, preferred_element_type=F32)
        new = [acc_ref[where[j]] + spread[:, j * tile : (j + 1) * tile] for j in range(per_row)]
        for j in range(per_row):
            acc_ref[where[j]] = new[j]
        return carry

    lax.fori_loop(first, last, step, 0, unroll=unroll)


def smooth_kernel(
    vertical_hbm, direction_hbm, members_hbm, residual_hbm, iterate_hbm, columns_hbm, tiles_hbm,
    members_ref, mixed_ref, residual_ref, iterate_ref, own_ref, band_ref, table_ref, smooth_ref, chip_ref, tiles_ref,
    vertical_ref, padded_ref, direction_ref, sems,
):
    mem_dev, lev_dev, points = members_ref.shape
    blocks, _, tile = smooth_ref.shape
    share = own_ref.shape[1]
    mine = pl.ds(pl.multiple_of(lax.axis_index("member") * share, share), share)
    pairs = [
        (vertical_hbm, vertical_ref),
        (direction_hbm, direction_ref),
        (members_hbm, members_ref),
        (columns_hbm, table_ref),
        (tiles_hbm.at[pl.ds(0, tiles_ref.shape[0])], tiles_ref),
        (direction_hbm.at[:, mine], own_ref),
        (residual_hbm, residual_ref),
        (iterate_hbm, iterate_ref),
    ]
    copies = [pltpu.make_async_copy(source, target, sems.at[i]) for i, (source, target) in enumerate(pairs)]
    for copy in copies:
        copy.start()
    width, levels = vertical_ref.shape
    slab = lax.axis_index("slab")
    level_start = slab * lev_dev
    even = slab % 2 == 0
    padded_ref[...] = jnp.zeros_like(padded_ref)
    copies[0].wait()
    for i in range(width):
        padded_ref[i : i + 1, LANES : LANES + levels] = vertical_ref[i : i + 1, :]
    total = padded_ref.shape[1]
    turned = pltpu.roll(padded_ref[...], total - (LANES - HALO + level_start), 1)[:, :LANES]
    band = jnp.concatenate([turned, jnp.zeros((LANES - turned.shape[0], LANES), F32)], axis=0).T
    inner, rim = level_matrix(band[: lev_dev + 2 * HALO], even, level_start, levels, lev_dev, mem_dev)
    band_ref[...] = split3(rim)
    copies[1].wait()
    copies[2].wait()

    def fields(cols):
        field = direction_ref[:, cols]
        wide = [members_ref[m, :, cols].astype(F32) * field for m in range(mem_dev)]
        low = jnp.concatenate([x[:HALO] for x in wide], axis=0)
        high = jnp.concatenate([x[lev_dev - HALO :] for x in wide], axis=0)
        chip_ref[:, cols] = jnp.where(even, high, low).astype(BF16)
        mixed = jnp.concatenate(wide, axis=0).astype(BF16)
        mixed_ref[:, cols] = mixed
        return mixed

    vertical_pass(split3(inner), fields, blocks, tile, smooth_ref)
    for copy in copies[3:]:
        copy.wait()


def interior_kernel(table_ref, smooth_ref, early_ref, tiles_hbm, late_ref, inner_ref, columns_ref, acc_ref, sems):
    early, late = early_ref.shape[0], late_ref.shape[0]
    part = late // LATE_CHUNKS
    copies = [
        pltpu.make_async_copy(
            tiles_hbm.at[pl.ds(early + i * part, part)], late_ref.at[pl.ds(i * part, part)], sems.at[i]
        )
        for i in range(LATE_CHUNKS)
    ]
    fetch = pltpu.make_async_copy(table_ref, columns_ref, sems.at[LATE_CHUNKS])
    fetch.start()
    for copy in copies:
        copy.start()
    acc_ref[...] = jnp.zeros_like(acc_ref)
    fetch.wait()
    adjoint_pass(0, early, 0, columns_ref, early_ref, smooth_ref, acc_ref, 8)
    for i, copy in enumerate(copies):
        copy.wait()
        adjoint_pass(early + i * part, early + (i + 1) * part, early, columns_ref, late_ref, smooth_ref, acc_ref, 8)
    inner_ref[...] = acc_ref[...].astype(BF16)


def forward_share(g, wide, base, columns_ref, tiles_ref, inner_ref, rim_ref, members_ref):
    mem_dev, lev_dev, points = members_ref.shape
    blocks, per_row, tile, _ = tiles_ref.shape
    middle = lev_dev - 2 * HALO
    pieces = []
    for k in range(wide):
        r = g * wide + k
        left = []
        for j in range(per_row):
            c = columns_ref[j, r]
            left.append(jnp.concatenate([inner_ref[c], rim_ref[c]], axis=0))
        right = jnp.concatenate([tiles_ref[r - base, j] for j in range(per_row)], axis=1)
        field = lax.dot_general(jnp.concatenate(left, axis=1), right, NT, preferred_element_type=F32)
        cols = pl.ds(pl.multiple_of(r * tile, tile), tile)
        total = jnp.zeros((lev_dev, tile), F32)
        for m in range(mem_dev):
            inside = field[m * middle : (m + 1) * middle]
            low = mem_dev * middle + 2 * m * HALO
            levels = jnp.concatenate([field[low : low + HALO], inside, field[low + HALO : low + 2 * HALO]], axis=0)
            total = total + members_ref[m, :, cols].astype(F32) * levels
        pieces.append(total)
    return jnp.concatenate(pieces, axis=1)


def forward_shares(shifts, columns_ref, early_ref, late_ref, inner_ref, rim_ref, members_ref, out_refs):
    far_count, _, share = out_refs[0].shape
    early = early_ref.shape[0]
    wide = share // early_ref.shape[3]
    here = lax.axis_index("member") % NEAR
    for shift, out_ref in zip(shifts, out_refs):
        target = (here + shift) % NEAR
        for z in range(far_count):
            in_early = (z + 1) * NEAR * wide <= early
            base, tiles_ref = (0, early_ref) if in_early else (early, late_ref)
            value = forward_share(z * NEAR + target, wide, base, columns_ref, tiles_ref, inner_ref, rim_ref, members_ref)
            out_ref[z] = value.astype(out_ref.dtype)


def product_kernel(
    table_ref, band_ref, members_ref, mixed_ref, inner_ref, chip_ref, link_ref, early_ref, late_ref,
    rim_ref, *rest, shifts,
):
    *out_refs, columns_ref, smooth_ref, acc_ref, sem = rest
    early, _, tile, _ = early_ref.shape
    blocks = early + late_ref.shape[0]
    fetch = pltpu.make_async_copy(table_ref, columns_ref, sem)
    fetch.start()

    def fields(cols):
        return jnp.concatenate([mixed_ref[:, cols], chip_ref[:, cols], link_ref[:, cols]], axis=0)

    vertical_pass(band_ref[...], fields, blocks, tile, smooth_ref, acc_ref)
    fetch.wait()
    adjoint_pass(0, early, 0, columns_ref, early_ref, smooth_ref, acc_ref, 16)
    adjoint_pass(early, blocks, early, columns_ref, late_ref, smooth_ref, acc_ref, 16)
    rim_ref[...] = acc_ref[...].astype(BF16)
    forward_shares(shifts, columns_ref, early_ref, late_ref, inner_ref, rim_ref, members_ref, out_refs)


def share_kernel(table_ref, members_ref, early_ref, late_ref, inner_ref, rim_ref, *rest, shifts):
    *out_refs, columns_ref, sem = rest
    fetch = pltpu.make_async_copy(table_ref, columns_ref, sem)
    fetch.start()
    fetch.wait()
    forward_shares(shifts, columns_ref, early_ref, late_ref, inner_ref, rim_ref, members_ref, out_refs)


def fold_kernel(own_ref, *refs):
    *arrived, out_ref = refs
    total = own_ref[...]
    for ref in arrived:
        total = total + ref[...].astype(F32)
    out_ref[...] = total.astype(out_ref.dtype)


def full_sum(value):
    return jnp.sum(jnp.sum(value, axis=0, keepdims=True), axis=1, keepdims=True)


def image_kernel(parts_ref, own_ref, residual_ref, image_ref, sums_ref, *, scale):
    total = parts_ref[0].astype(F32)
    for i in range(1, parts_ref.shape[0]):
        total = total + parts_ref[i].astype(F32)
    own = own_ref[...]
    residual = residual_ref[...]
    image = own + total / scale
    image_ref[...] = image
    rr = full_sum(residual * residual)
    di = full_sum(own * image)
    ii = full_sum(image * image)
    ri = full_sum(residual * image)
    guess = jnp.where(ii > 0.0, ri / jnp.where(ii > 0.0, ii, 1.0), 0.0)
    left = residual - guess * image
    ll = full_sum(left * left)
    li = full_sum(left * image)
    lane = lax.broadcasted_iota(jnp.int32, (1, sums_ref.shape[1]), 1)
    row = jnp.zeros(lane.shape, F32)
    for k, value in enumerate((rr, di, ll, li, ii, guess)):
        row = jnp.where(lane == k, value, row)
    sums_ref[...] = jnp.broadcast_to(row, sums_ref.shape)


def update_kernel(parts_ref, own_ref, residual_ref, iterate_ref, image_ref, x_ref, r_ref, d_ref):
    parts = parts_ref[...]
    sums = jnp.sum(parts, axis=0, keepdims=True)
    norm_old = sums[:, 0:1]
    alpha = norm_old / sums[:, 1:2]
    ll, li, ii, guess = (parts[:, k : k + 1] for k in range(2, 6))
    shift = guess - alpha
    norm_new = jnp.sum(ll + shift * (2.0 * li + shift * ii), axis=0, keepdims=True)
    own = own_ref[...]
    residual_new = residual_ref[...] - alpha * image_ref[...]
    x_ref[...] = iterate_ref[...] + alpha * own
    r_ref[...] = residual_new
    d_ref[...] = residual_new + (norm_new / norm_old) * own


def on_device(members, direction, residual, iterate, tiles, columns, vertical):
    mem_dev, lev_dev, points = members.shape
    blocks, per_row, tile = tiles.shape[:3]
    vectors = mem_dev * lev_dev
    groups, slabs = lax.axis_size("member"), lax.axis_size("slab")
    share = points // groups
    member_count = mem_dev * groups
    levels, width = vertical.shape
    square = (lev_dev, share)
    edge = (mem_dev * HALO, points)

    far = functools.partial(pltpu.with_memory_space_constraint, memory_space=pltpu.HBM)
    near = functools.partial(pltpu.with_memory_space_constraint, memory_space=pltpu.VMEM)
    limit = pltpu.CompilerParams(vmem_limit_bytes=32 * 2**20)
    to_link, = pl.pallas_call(
        link_kernel,
        out_shape=(pltpu.VMEM(edge, BF16),),
        in_specs=[HBM, HBM],
        out_specs=(VMEM,),
        scratch_shapes=[
            pltpu.VMEM((mem_dev, 2 * HALO, points), BF16),
            pltpu.VMEM((HALO, points), F32),
            pltpu.SemaphoreType.DMA((2 * EDGE_CHUNKS,)),
        ],
        compiler_params=limit,
        name="link_edge",
    )(far(members), far(direction))
    pairs = [(i, (i + 1) % slabs) for i in range(1, slabs, 2)]
    link = lax.ppermute(to_link, "slab", pairs + [(target, source) for source, target in pairs])

    rim_rows = 2 * mem_dev * HALO
    inner_rows = vectors - rim_rows
    columns_scratch = pltpu.SMEM((per_row, blocks), jnp.int32)
    early = EARLY_SHARE * blocks // 8
    late = blocks - early
    (
        members_near, mixed, residual_near, iterate_near, own, band, columns_near, smooth, to_chip, tiles_early,
    ) = pl.pallas_call(
        smooth_kernel,
        out_shape=(
            pltpu.VMEM(members.shape, BF16), pltpu.VMEM((vectors, points), BF16),
            pltpu.VMEM(square, F32), pltpu.VMEM(square, F32), pltpu.VMEM(square, F32),
            pltpu.VMEM((3 * rim_rows, vectors + rim_rows), BF16),
            pltpu.VMEM((per_row, blocks), jnp.int32),
            pltpu.VMEM((blocks, inner_rows, tile), BF16),
            pltpu.VMEM(edge, BF16),
            pltpu.VMEM((early,) + tiles.shape[1:], BF16),
        ),
        in_specs=[HBM] * 7,
        out_specs=(VMEM,) * 10,
        scratch_shapes=[
            pltpu.VMEM((width, levels), F32),
            pltpu.VMEM((-(-width // 8) * 8, levels + 2 * LANES), F32),
            pltpu.VMEM(direction.shape, F32),
            pltpu.SemaphoreType.DMA((8,)),
        ],
        compiler_params=limit,
        cost_estimate=pl.CostEstimate(flops=0, bytes_accessed=tiles.size // 2, transcendentals=0),
        name="smooth",
    )(far(vertical.T), far(direction), far(members), far(residual), far(iterate), far(columns.T), far(tiles))
    chip = lax.ppermute(to_chip, "slab", [(i, i ^ 1) for i in range(slabs)])
    tiles_late, inner = pl.pallas_call(
        interior_kernel,
        out_shape=(pltpu.VMEM((late,) + tiles.shape[1:], BF16), pltpu.VMEM((blocks, inner_rows, tile), BF16)),
        in_specs=[VMEM] * 3 + [HBM],
        out_specs=(VMEM,) * 2,
        scratch_shapes=[
            columns_scratch,
            pltpu.VMEM((blocks, inner_rows, tile), F32),
            pltpu.SemaphoreType.DMA((LATE_CHUNKS + 1,)),
        ],
        compiler_params=limit,
        cost_estimate=pl.CostEstimate(
            flops=2 * inner_rows * points * per_row * tile, bytes_accessed=2 * tiles.size * 2, transcendentals=0
        ),
        name="interior",
    )(columns_near, smooth, tiles_early, far(tiles))

    far_count = groups // NEAR
    piece = (far_count, lev_dev, share)
    flops = 2 * vectors * points * per_row * tile

    def shares(shifts, dtype, name):
        return pl.pallas_call(
            functools.partial(share_kernel, shifts=shifts),
            out_shape=(pltpu.VMEM(piece, dtype),) * len(shifts),
            in_specs=[VMEM] * 6,
            out_specs=(VMEM,) * len(shifts),
            scratch_shapes=[columns_scratch, pltpu.SemaphoreType.DMA],
            compiler_params=limit,
            cost_estimate=pl.CostEstimate(
                flops=flops * len(shifts) // NEAR, bytes_accessed=tiles.size * 2 * len(shifts) // NEAR, transcendentals=0
            ),
            name=name,
        )(columns_near, members_near, tiles_early, tiles_late, inner, rim)

    def send(value, shift):
        return lax.ppermute(value, "member", [(i, i // NEAR * NEAR + (i + shift) % NEAR) for i in range(groups)])

    early, late = (1, 3, 2), ()
    rim, *sent = pl.pallas_call(
        functools.partial(product_kernel, shifts=early),
        out_shape=(pltpu.VMEM((blocks, rim_rows, tile), BF16),) + (pltpu.VMEM(piece, BF16),) * len(early),
        in_specs=[VMEM] * 9,
        out_specs=(VMEM,) * (1 + len(early)),
        scratch_shapes=[
            columns_scratch,
            pltpu.VMEM((blocks, rim_rows, tile), BF16),
            pltpu.VMEM((blocks, rim_rows, tile), F32),
            pltpu.SemaphoreType.DMA,
        ],
        compiler_params=limit,
        name="product",
    )(columns_near, band, members_near, mixed, inner, chip, link, tiles_early, tiles_late)
    arrived = [send(value, shift) for value, shift in zip(sent, early)]
    own_part, = shares((0,), F32, "own")
    folded = pl.pallas_call(
        fold_kernel,
        out_shape=pltpu.VMEM(piece, BF16),
        in_specs=[VMEM] * NEAR,
        out_specs=VMEM,
        compiler_params=limit,
        name="fold",
    )(near(own_part), *(near(x) for x in arrived))
    columns_of = [[y + NEAR * z for z in range(far_count)] for y in range(NEAR)]
    parts = lax.all_to_all(folded, "member", 0, 0, axis_index_groups=columns_of, tiled=True)
    devices = groups * slabs
    image, sums = pl.pallas_call(
        functools.partial(image_kernel, scale=float(member_count - 1)),
        out_shape=(pltpu.VMEM(square, F32), pltpu.VMEM((devices, 128), F32)),
        in_specs=[VMEM] * 3,
        out_specs=(VMEM,) * 2,
        compiler_params=limit,
        name="image",
    )(near(parts), own, residual_near)

    spread = lax.all_to_all(
        sums.reshape(devices, 1, 128), ("member", "slab"), 0, 0, axis_index_groups=[list(range(devices))[::-1]], tiled=True
    )
    field = jax.ShapeDtypeStruct(square, F32)
    return pl.pallas_call(
        update_kernel,
        out_shape=(field, field, field),
        in_specs=[VMEM] * 5,
        out_specs=(VMEM,) * 3,
        compiler_params=limit,
        name="update",
    )(near(spread.reshape(devices, 128)), own, residual_near, iterate_near, image)


def solution(mesh):
    placed = (
        P("member", "slab", None),
        P("slab", None),
        P("slab", "member"),
        P("slab", "member"),
        P(),
        P(),
        P(),
    )
    return jax.shard_map(
        on_device,
        mesh=mesh,
        in_specs=placed,
        out_specs=(P("slab", "member"), P("slab", "member"), P("slab", "member")),
        check_vma=False,
    )
```
